128 devices in a mesh: lat: 32 (over z, x, core), lon: 4 (over y).
Axes of the slice: x: 4, y: 4, z: 4, core: 2. Of those that a mesh axis runs over, the one named last changes fastest.
Arguments:
- grid_in: bfloat16 [131072, 227], P(('lat', 'lon')), may hold values from -6 to 6
- g2m_senders: int32 [98304], P(('lat', 'lon')), may hold values from 0 to 1023
- g2m_dest: int32 [98304, 1], P(('lat', 'lon')), may hold values from 0 to 8; in each aligned block of 768 rows (0 to 767, 768 to 1535, ...) at most 192 rows name the same one
- g2m_receivers: int32 [98304], P(('lat', 'lon')), may hold values from 0 to 319
- g2m_feat: bfloat16 [4, 98304], P(None, ('lat', 'lon')), may hold values from -6 to 6
- halo_near: int32 [128, 8, 64], P(('lat', 'lon')), may hold values from 0 to 319
- halo_far: int32 [128, 128, 2], P(('lat', 'lon')), may hold values from 0 to 319
- mesh_senders: int32 [327680], P(('lat', 'lon')), may hold values from 0 to 1087
- mesh_receivers: int32 [327680], P(('lat', 'lon')), may hold values from 0 to 319
- mesh_feat: bfloat16 [4, 327680], P(None, ('lat', 'lon')), may hold values from -6 to 6
- w_grid_in: bfloat16 [227, 512], replicated, may hold values from -0.375 to 0.375
- w_grid_out: bfloat16 [512, 512], replicated, may hold values from -0.25 to 0.25
- w_edge_latent: bfloat16 [512, 512], replicated, may hold values from -0.25 to 0.25
- w_edge_feat: bfloat16 [4, 512], replicated, may hold values from -3 to 3
- w_edge_out: bfloat16 [512, 512], replicated, may hold values from -0.25 to 0.25
- w_node_in: bfloat16 [512, 512], replicated, may hold values from -0.25 to 0.25
- w_node_out: bfloat16 [512, 512], replicated, may hold values from -0.25 to 0.25
- w_mesh_feat: bfloat16 [4, 512], replicated, may hold values from -3 to 3
- w_proc_edge: bfloat16 [512, 512], replicated, may hold values from -0.25 to 0.25
- w_proc_send: bfloat16 [512, 512], replicated, may hold values from -0.25 to 0.25
- w_proc_recv: bfloat16 [512, 512], replicated, may hold values from -0.25 to 0.25
- w_proc_out: bfloat16 [512, 512], replicated, may hold values from -0.25 to 0.25
- w_upd_self: bfloat16 [512, 512], replicated, may hold values from -0.25 to 0.25
- w_upd_sum: bfloat16 [512, 512], replicated, may hold values from -0.25 to 0.25
- w_upd_out: bfloat16 [512, 512], replicated, may hold values from -0.25 to 0.25
Outputs:
- mesh_out: bfloat16 [40960, 512], P(('lat', 'lon'))
- edge_out: bfloat16 [327680, 512], P(('lat', 'lon'))
The draws below stay inside these ranges and needn't reach their ends.
Inputs may be any that keep to these rules, and one draw needn't show every extreme that they name: `g2m_dest`: at most 192 of one device's grid-to-mesh edges name the same code; in every draw some code is named by exactly 192 of some device's edges.
All inputs are finite; a program needn't handle non-finite values.
Results may differ from the reference program's by a relative error of at most 0.017.
Values may be sent and summed in bfloat16 or wider, within the bound.
A program may use at most 128 MiB of HBM per device.

```python
import math
import jax
import jax.numpy as jnp
import numpy as np
from jax import lax

L = 512
CIN = 227
EF = 4
GRID_DEV = 1024
G2M_DEV = 768
MESH_DEV = 320
MESH_E_DEV = 2560
HCAP = 64
FCAP = 2
CAP = 192
GRID = 131072
G2M = 98304
MESH_E = 327680
N_LAT = 32
N_LON = 4


def draw_mesh_senders(key, part):
    key = jax.random.fold_in(key, 7)
    category_key, own_key, near_key, far_key = jax.random.split(key, 4)
    category = jax.random.randint(category_key, (MESH_E,), 0, 10)
    own_pick = jax.random.randint(own_key, (MESH_E,), 0, MESH_DEV)
    near_pick = MESH_DEV + jax.random.randint(near_key, (MESH_E,), 0, 8 * HCAP)
    far_pick = MESH_DEV + 8 * HCAP + jax.random.randint(far_key, (MESH_E,), 0, N_LAT * N_LON * FCAP)
    chosen = jnp.where(category < 4, own_pick, jnp.where(category < 9, near_pick, far_pick))
    return chosen.astype(jnp.int32)


def touch_ends(values, stream_key, low, top_value):
    longest = values.shape.index(max(values.shape))
    spots = []
    for shift in (0, 1):
        where = [jax.random.randint(jax.random.fold_in(stream_key, axis), (), 0, length) for axis, length in enumerate(values.shape)]
        where[longest] = (where[longest] + shift) % values.shape[longest]
        spots.append(tuple(where))
    return values.at[spots[0]].set(low).at[spots[1]].set(top_value)


def levels(rng, dims, pieces, low, top_value):
    def one(dim, parts):
        draws = jax.random.uniform(jax.random.fold_in(jax.random.fold_in(rng, 6), dim), (parts,), jnp.float32, low / len(pieces), top_value / len(pieces))
        return jnp.repeat(jnp.exp(draws), dims[dim] // parts).reshape((-1,) + (1,) * (len(dims) - dim - 1))

    level = one(*pieces[0])
    for cut in pieces[1:]:
        level = level * one(*cut)
    return level


def routed_block(rng, own, number, rows, count, top, reach, slope):
    ranking = jax.random.permutation(rng, count)
    heavy_load, usual = portions_of(count, rows * top, reach, slope, True), portions_of(count, rows * top, reach, slope, False)
    places = jnp.arange(count)

    def named(sizes, offset_by):
        used = int((sizes > 0).sum())
        fixed = max(1, used // 4)
        shifted = fixed + (places - fixed + offset_by * (used - fixed)) % max(1, count - fixed)
        return jnp.zeros((count,), jnp.int32).at[ranking[jnp.where(places < fixed, places, shifted)]].set(jnp.asarray(sizes, jnp.int32))

    sizes = jnp.where(number % 4 == 0, named(heavy_load, number // 4), named(usual, number - number // 4 - 1))
    mixed = jax.random.permutation(jax.random.fold_in(own, 3), count)
    donor, taker = mixed[0:count // 2 * 2:2], mixed[1:count // 2 * 2:2]
    room = jnp.minimum(sizes[donor] - 1, reach - sizes[taker]) // 2
    room = jnp.where((donor == ranking[0]) | (taker == ranking[0]) | (sizes[taker] == 0), 0, jnp.maximum(room, 0))
    shifted = jax.random.randint(jax.random.fold_in(own, 4), (count // 2,), 0, 1 << 20) % (room + 1)
    sizes = sizes.at[donor].add(-shifted).at[taker].add(shifted)
    labels = jnp.searchsorted(jnp.cumsum(sizes), jnp.arange(rows * top), side="right").astype(jnp.int32)
    table = labels.reshape(top, rows).T
    table = table[jax.random.permutation(jax.random.fold_in(own, 1), rows)]
    offset_by = jax.random.randint(jax.random.fold_in(own, 2), (rows, 1), 0, top)
    return jnp.take_along_axis(table, (jnp.arange(top)[None, :] + offset_by) % top, axis=1)


def portions_of(count, total, limit, lean, full):
    portions = [(1 << 20) // math.isqrt(rank ** lean) + 1 for rank in range(1, count + 1)]
    largest = limit if full else min(limit, max(-(-total // count), total * portions[0] // sum(portions)))
    least = 1 if total - largest >= count - 1 else 0
    holding, spare = [largest] + [least] * (count - 1), total - largest - least * (count - 1)
    while spare > 0:
        free = [i for i in range(1, count) if holding[i] < largest] or [i for i in range(1, count) if holding[i] < limit]
        whole, budget = sum([portions[i] for i in free]), spare
        for i in free:
            extra = min(limit - holding[i], max(1, budget * portions[i] // whole), spare)
            holding[i] = holding[i] + extra
            spare = spare - extra
    return np.array(holding)


def scatter_about(rng, dims, deviation, bound, cuts=(), held_as=jnp.bfloat16):
    gain = levels(rng, dims, cuts, -0.22, 0.18) if cuts else 1.0
    result = jax.random.normal(rng, dims, jnp.float32) * deviation * gain
    return jnp.minimum(jnp.maximum(result, -bound), bound).astype(held_as)


def setup_inputs(seed: int = 0) -> dict:
    arg_keys = jax.random.split(jax.random.key(seed), 26)
    grid_in = scatter_about(arg_keys[0], (GRID, CIN), 1.0, 6.0, ((0, 128),))
    g2m_senders = touch_ends(jax.random.randint(arg_keys[1], (G2M,), 0, GRID_DEV), jax.random.fold_in(arg_keys[1], 1), 0, GRID_DEV - 1).astype(jnp.int32)
    g2m_dest_keys = jax.random.split(jax.random.fold_in(arg_keys[2], 1), G2M // G2M_DEV)
    g2m_dest_turns = jax.random.permutation(jax.random.fold_in(arg_keys[2], 3), G2M // G2M_DEV)
    g2m_dest = jax.vmap(lambda own, number: routed_block(jax.random.fold_in(arg_keys[2], 2), own, number, G2M_DEV, 9, 1, CAP, 2))(g2m_dest_keys, g2m_dest_turns).reshape((G2M, 1))
    g2m_receivers = touch_ends(jax.random.randint(arg_keys[3], (G2M,), 0, MESH_DEV), jax.random.fold_in(arg_keys[3], 1), 0, MESH_DEV - 1).astype(jnp.int32)
    g2m_feat = scatter_about(arg_keys[4], (EF, G2M), 1.0, 6.0, ((1, 128),))
    halo_near = touch_ends(jax.random.randint(arg_keys[5], (N_LAT * N_LON, 8, HCAP), 0, MESH_DEV), jax.random.fold_in(arg_keys[5], 1), 0, MESH_DEV - 1).astype(jnp.int32)
    halo_far = touch_ends(jax.random.randint(arg_keys[6], (N_LAT * N_LON, N_LAT * N_LON, FCAP), 0, MESH_DEV), jax.random.fold_in(arg_keys[6], 1), 0, MESH_DEV - 1).astype(jnp.int32)
    mesh_senders = draw_mesh_senders(jax.random.fold_in(arg_keys[25], 71), 0)
    mesh_receivers = touch_ends(jax.random.randint(arg_keys[8], (MESH_E,), 0, MESH_DEV), jax.random.fold_in(arg_keys[8], 1), 0, MESH_DEV - 1).astype(jnp.int32)
    mesh_feat = scatter_about(arg_keys[9], (EF, MESH_E), 1.0, 6.0, ((1, 128),))
    w_grid_in = scatter_about(arg_keys[10], (CIN, L), CIN ** -0.5, 0.375)
    w_grid_out = scatter_about(arg_keys[11], (L, L), L ** -0.5, 0.25)
    w_edge_latent = scatter_about(arg_keys[12], (L, L), L ** -0.5, 0.25)
    w_edge_feat = scatter_about(arg_keys[13], (EF, L), EF ** -0.5, 3.0)
    w_edge_out = scatter_about(arg_keys[14], (L, L), L ** -0.5, 0.25)
    w_node_in = scatter_about(arg_keys[15], (L, L), L ** -0.5, 0.25)
    w_node_out = scatter_about(arg_keys[16], (L, L), L ** -0.5, 0.25)
    w_mesh_feat = scatter_about(arg_keys[17], (EF, L), EF ** -0.5, 3.0)
    w_proc_edge = scatter_about(arg_keys[18], (L, L), L ** -0.5, 0.25)
    w_proc_send = scatter_about(arg_keys[19], (L, L), L ** -0.5, 0.25)
    w_proc_recv = scatter_about(arg_keys[20], (L, L), L ** -0.5, 0.25)
    w_proc_out = scatter_about(arg_keys[21], (L, L), L ** -0.5, 0.25)
    w_upd_self = scatter_about(arg_keys[22], (L, L), L ** -0.5, 0.25)
    w_upd_sum = scatter_about(arg_keys[23], (L, L), L ** -0.5, 0.25)
    w_upd_out = scatter_about(arg_keys[24], (L, L), L ** -0.5, 0.25)
    return {"grid_in": grid_in, "g2m_senders": g2m_senders, "g2m_dest": g2m_dest, "g2m_receivers": g2m_receivers, "g2m_feat": g2m_feat, "halo_near": halo_near, "halo_far": halo_far, "mesh_senders": mesh_senders, "mesh_receivers": mesh_receivers, "mesh_feat": mesh_feat, "w_grid_in": w_grid_in, "w_grid_out": w_grid_out, "w_edge_latent": w_edge_latent, "w_edge_feat": w_edge_feat, "w_edge_out": w_edge_out, "w_node_in": w_node_in, "w_node_out": w_node_out, "w_mesh_feat": w_mesh_feat, "w_proc_edge": w_proc_edge, "w_proc_send": w_proc_send, "w_proc_recv": w_proc_recv, "w_proc_out": w_proc_out, "w_upd_self": w_upd_self, "w_upd_sum": w_upd_sum, "w_upd_out": w_upd_out}


def normalize(values):
    row_mean = lax.optimization_barrier(jnp.mean(values, axis=-1, keepdims=True))
    centred = values - row_mean
    spread = lax.optimization_barrier(jnp.mean(centred * centred, axis=-1, keepdims=True))
    return centred * lax.rsqrt(spread + 1e-05)

def product(left, right):
    return jnp.dot(left, right, preferred_element_type=jnp.float32)

def neighbour(owner, code):
    lat_index = owner // N_LON
    lon_index = owner % N_LON
    lat_new = (lat_index + code // 3 - 1) % N_LAT
    lon_new = (lon_index + code % 3 - 1) % N_LON
    return (lat_new * N_LON + lon_new).astype(jnp.int32)

def reference(grid_in, g2m_senders, g2m_dest, g2m_receivers, g2m_feat, halo_near, halo_far, mesh_senders, mesh_receivers, mesh_feat, w_grid_in, w_grid_out, w_edge_latent, w_edge_feat, w_edge_out, w_node_in, w_node_out, w_mesh_feat, w_proc_edge, w_proc_send, w_proc_recv, w_proc_out, w_upd_self, w_upd_sum, w_upd_out):
    devices = N_LAT * N_LON
    codes_all = g2m_dest[:, 0]

    def grid_block(totals, block_index):
        grid_rows = lax.dynamic_slice_in_dim(grid_in, block_index * GRID_DEV, GRID_DEV, 0)
        grid_hidden = jax.nn.silu(product(grid_rows, w_grid_in)).astype(jnp.bfloat16)
        grid_latent = normalize(product(grid_hidden, w_grid_out)).astype(jnp.bfloat16)
        start = block_index * G2M_DEV
        senders = lax.dynamic_slice_in_dim(g2m_senders, start, G2M_DEV, 0)
        codes = lax.dynamic_slice_in_dim(codes_all, start, G2M_DEV, 0)
        receivers = lax.dynamic_slice_in_dim(g2m_receivers, start, G2M_DEV, 0)
        features = lax.dynamic_slice_in_dim(g2m_feat, start, G2M_DEV, 1)
        summed_in = product(grid_latent[senders], w_edge_latent) + product(features.T, w_edge_feat)
        edge_hidden = jax.nn.silu(summed_in).astype(jnp.bfloat16)
        message = normalize(product(edge_hidden, w_edge_out)).astype(jnp.bfloat16)
        node_ids = (neighbour(block_index, codes) * MESH_DEV + receivers).astype(jnp.int32)
        totals = totals.at[node_ids].add(message.astype(jnp.float32))
        return (totals, None)
    totals, _ = lax.scan(grid_block, jnp.zeros((devices * MESH_DEV, L), jnp.float32), jnp.arange(devices, dtype=jnp.int32))
    mesh_sum = totals.astype(jnp.bfloat16)
    node_hidden = jax.nn.silu(product(mesh_sum, w_node_in)).astype(jnp.bfloat16)
    mesh_latent = normalize(product(node_hidden, w_node_out)).astype(jnp.bfloat16)
    edge_rows = jnp.arange(devices * MESH_E_DEV, dtype=jnp.int32)
    owner = (edge_rows // MESH_E_DEV).astype(jnp.int32)
    near_q = jnp.clip(mesh_senders - MESH_DEV, 0, 8 * HCAP - 1).astype(jnp.int32)
    near_code = near_q // HCAP
    near_slot = near_q % HCAP
    full_code = jnp.where(near_code < 4, near_code, near_code + 1).astype(jnp.int32)
    near_patch = neighbour(owner, full_code)
    back_full = 8 - full_code
    back_code = jnp.where(back_full < 4, back_full, back_full - 1).astype(jnp.int32)
    near_node = near_patch * MESH_DEV + halo_near[near_patch, back_code, near_slot]
    far_q = jnp.clip(mesh_senders - MESH_DEV - 8 * HCAP, 0, devices * FCAP - 1).astype(jnp.int32)
    far_patch = far_q // FCAP
    far_node = far_patch * MESH_DEV + halo_far[far_patch, owner, far_q % FCAP]
    own_node = owner * MESH_DEV + mesh_senders
    sources = jnp.where(mesh_senders < MESH_DEV, own_node, jnp.where(mesh_senders < MESH_DEV + 8 * HCAP, near_node, far_node)).astype(jnp.int32)

    def mesh_block(block_index):
        start = block_index * MESH_E_DEV
        block_sources = lax.dynamic_slice_in_dim(sources, start, MESH_E_DEV, 0)
        receivers = lax.dynamic_slice_in_dim(mesh_receivers, start, MESH_E_DEV, 0)
        features = lax.dynamic_slice_in_dim(mesh_feat, start, MESH_E_DEV, 1)
        own_nodes = lax.dynamic_slice_in_dim(mesh_latent, block_index * MESH_DEV, MESH_DEV, 0)
        edge_embed = product(features.T, w_mesh_feat).astype(jnp.bfloat16)
        summed_in = product(edge_embed, w_proc_edge) + product(mesh_latent[block_sources], w_proc_send) + product(own_nodes[receivers], w_proc_recv)
        proc_hidden = jax.nn.silu(summed_in).astype(jnp.bfloat16)
        edge_out = (edge_embed.astype(jnp.float32) + normalize(product(proc_hidden, w_proc_out))).astype(jnp.bfloat16)
        edge_sum = jax.ops.segment_sum(edge_out.astype(jnp.float32), receivers, num_segments=MESH_DEV).astype(jnp.bfloat16)
        node_update = jax.nn.silu(product(own_nodes, w_upd_self) + product(edge_sum, w_upd_sum)).astype(jnp.bfloat16)
        mesh_out = (own_nodes.astype(jnp.float32) + normalize(product(node_update, w_upd_out))).astype(jnp.bfloat16)
        return (edge_out, mesh_out)
    edge_blocks, mesh_blocks = lax.map(mesh_block, jnp.arange(devices, dtype=jnp.int32))
    return (mesh_blocks.reshape(devices * MESH_DEV, L), edge_blocks.reshape(devices * MESH_E_DEV, L))
```

```python
import functools

import jax
import jax.numpy as jnp
from jax import lax
from jax.experimental import pallas as pl
from jax.experimental.pallas import tpu as pltpu
from jax.sharding import PartitionSpec as P

F32 = jnp.float32
BF16 = jnp.bfloat16
I32 = jnp.int32
MESH = pl.DeviceIdType.MESH

N_LAT, N_LON = 32, 4
L = 512
CIN = 227
GRID_N = 1024
EDGES = 768
NODES = 320
MEDGES = 2560
CAP = 192
HCAP = 64
SLOT = CAP + 16
BLK = 256
NBLK = MEDGES // BLK

CODES = (1, 7, 3, 5, 0, 2, 6, 8)
SEND_ORDER = (4, 5, 6, 7, 2, 3, 0, 1)

COL_SEND = 0
COL_NEAR = 6
COL_FAR = 10
COL_MS = 12
COL_MR = 32

W_NAMES = (
    "wgo", "wel", "weo", "wni", "wno", "wpe", "wps", "wpr", "wpo", "wus", "wua", "wuo",
)


def dot(a, b):
    return jnp.dot(a, b, preferred_element_type=F32)


def dot_tn(a, b):
    return lax.dot_general(a, b, (((0,), (0,)), ((), ())), preferred_element_type=F32)


def dot_nt(a, b):
    return lax.dot_general(a, b, (((1,), (1,)), ((), ())), preferred_element_type=F32)


def silu(v):
    h = 0.5 * v
    return h + h * jnp.tanh(h)


def scaled(v):
    return v * lax.rsqrt(jnp.mean(v * v, axis=-1, keepdims=True) + 1e-05)


def normalize(v):
    c = v - jnp.mean(v, axis=-1, keepdims=True)
    return c * lax.rsqrt(jnp.mean(c * c, axis=-1, keepdims=True) + 1e-05)


def iota(shape, dim):
    return lax.broadcasted_iota(I32, shape, dim)


def hot(mask):
    return jnp.where(mask, 1.0, 0.0).astype(BF16)


def kernel(
    grid_hbm, idx_ref, dest_ref, recv_ref, gfeat_ref, mrow_ref, mfeat_ref, wgi_hbm, wef_ref, wmf_ref,
    wgo_h, wel_h, weo_h, wni_h, wno_h, wpe_h, wps_h, wpr_h, wpo_h, wus_h, wua_h, wuo_h,
    mesh_out, edge_out,
    graw, gsel, wraw, wpad32, wgi, wts, aux, wefp, featp, wcat,
    eout, ein, scol, rcol, apre, apost, rmask, gsend,
    tpre, tpost, near_out, a_out, a_in, b_out, pre, obuf, lat_buf, mbuf,
    in_sem, w_sem, es_sem, er_sem, ns_sem, nr_sem, as_sem, ar_sem, bs_sem, br_sem, o_sem,
):
    lat = lax.axis_index("lat")
    lon = lax.axis_index("lon")
    zx = lax.div(lat, 2)
    core = lax.rem(lat, 2)
    spot = core * 4 + lon

    def near_id(code):
        return (
            lax.rem(lat + (code // 3 - 1) + N_LAT, N_LAT),
            lax.rem(lon + (code % 3 - 1) + N_LON, N_LON),
        )

    def a_peer(i):
        other = lax.rem(zx + i, 16)
        return other, (other * 2 + core, lon)

    def b_peer(i):
        other = lax.rem(spot + i, 8)
        return other, (zx * 2 + lax.div(other, 4), lax.rem(other, 4))

    barrier = pltpu.get_barrier_semaphore()
    for code in CODES:
        pl.semaphore_signal(barrier, inc=1, device_id=near_id(code), device_id_type=MESH)

    def greet_a(i, carry):
        pl.semaphore_signal(barrier, inc=1, device_id=a_peer(i)[1], device_id_type=MESH)
        return carry

    def greet_b(i, carry):
        pl.semaphore_signal(barrier, inc=1, device_id=b_peer(i)[1], device_id_type=MESH)
        return carry

    lax.fori_loop(1, 16, greet_a, 0)
    lax.fori_loop(1, 8, greet_b, 0)

    g_copy = pltpu.make_async_copy(grid_hbm, graw, in_sem.at[0])
    g_copy.start()
    wi_copy = pltpu.make_async_copy(wgi_hbm, wraw, in_sem.at[1])
    wi_copy.start()
    w_copies = {}
    for k, (name, ref) in enumerate(
        zip(W_NAMES, (wgo_h, wel_h, weo_h, wni_h, wno_h, wpe_h, wps_h, wpr_h, wpo_h, wus_h, wua_h, wuo_h))
    ):
        w_copies[name] = pltpu.make_async_copy(ref, wts.at[k], w_sem.at[k])
        w_copies[name].start()

    def weight(name):
        return wts[W_NAMES.index(name)]

    codes = dest_ref[...]
    marks = jnp.where(iota((16, EDGES), 0) == codes, 1.0, 0.0)
    below = hot(iota((EDGES, EDGES), 0) < iota((EDGES, EDGES), 1))
    earlier = dot(marks.astype(BF16), below)
    rank = jnp.sum(earlier * marks, axis=0, keepdims=True).astype(I32)
    place = codes * CAP + rank

    name_row = recv_ref[...] + 1
    aux[...] = jnp.zeros_like(aux)
    aux[0:1, :] = lax.shift_right_logical(name_row, 4).astype(F32)
    aux[1:2, :] = lax.bitwise_and(name_row, 15).astype(F32)
    aux[4:8, :] = gfeat_ref[...].astype(F32)
    aux_rows = aux[...].astype(BF16)

    idx_t = jnp.transpose(idx_ref[...])

    g_copy.wait()
    gsel[:, 128:256] = jnp.zeros((EDGES, 128), BF16)
    for b in range(EDGES // 128):
        pick = hot(idx_t[:, COL_SEND + b : COL_SEND + b + 1] == iota((128, GRID_N), 1))
        gsel[b * 128 : (b + 1) * 128, 0:CIN] = dot(pick, graw[...]).astype(BF16)

    def pack(code, target, k):
        choose = hot(iota((CAP, EDGES), 0) + code * CAP == place)
        target[k, 0:CAP, :] = dot(choose, gsel[...]).astype(BF16)
        target[k, CAP:SLOT, :] = jnp.zeros((16, 256), BF16)
        target[k, CAP:SLOT, 0:CAP] = dot_nt(aux_rows, choose).astype(BF16)

    def edge_copy(k):
        return pltpu.make_async_remote_copy(
            src_ref=eout.at[k],
            dst_ref=ein.at[k],
            send_sem=es_sem.at[k],
            recv_sem=er_sem.at[k],
            device_id=near_id(CODES[k]),
            device_id_type=MESH,
        )

    for n, k in enumerate(SEND_ORDER):
        pack(CODES[k], eout, k)
        if n == 0:
            pl.semaphore_wait(barrier, 8 + 15 + 7)
        edge_copy(k).start()
    pack(4, ein, 8)

    wi_copy.wait()
    wpad32[224:256, :] = jnp.zeros((32, L), F32)
    wpad32[0:CIN, :] = wraw[...].astype(F32)
    wgi[...] = wpad32[...].astype(BF16)
    wefp[...] = jnp.zeros_like(wefp)
    wefp[4:8, :] = wef_ref[...].astype(F32)

    def centre(name):
        w_copies[name].wait()
        w = weight(name).astype(F32)
        wts[W_NAMES.index(name)] = (w - jnp.mean(w, axis=-1, keepdims=True)).astype(BF16)

    centre("wgo")
    w_copies["wel"].wait()
    centre("weo")

    def encode(slots, count):
        x = slots[:, 0:CAP, :].reshape(count * CAP, 256)
        h = silu(dot(x, wgi[...])).astype(BF16)
        latent = scaled(dot(h, weight("wgo"))).astype(BF16)
        wf = wefp[...].astype(BF16)
        tails = [slots[i, CAP:SLOT, :][:, 0:CAP] for i in range(count)]
        feat_part = jnp.concatenate([dot_tn(t, wf) for t in tails], axis=0) if count > 1 else dot_tn(tails[0], wf)
        h = silu(dot(latent, weight("wel")) + feat_part).astype(BF16)
        message = scaled(dot(h, weight("weo"))).astype(BF16)
        total = None
        for i in range(count):
            t = tails[i].astype(F32)
            node = (t[0:1, :] * 16.0 + t[1:2, :] - 1.0).astype(I32)
            part = dot(hot(iota((NODES, CAP), 0) == node), message[i * CAP : (i + 1) * CAP])
            total = part if total is None else total + part
        return total

    mbuf[...] = encode(ein[8:9], 1)

    for b in range(MEDGES // 128):
        scol[b] = jnp.broadcast_to(idx_t[:, COL_MS + b : COL_MS + b + 1], (128, 128))
        rcol[b] = jnp.broadcast_to(idx_t[:, COL_MR + b : COL_MR + b + 1], (128, 128))
    for b in range(6):
        gsend[b * 128 : (b + 1) * 128, :] = hot(idx_t[:, COL_NEAR + b : COL_NEAR + b + 1] == iota((128, NODES), 1))

    featp[...] = jnp.zeros_like(featp)
    featp[0:4, :] = mfeat_ref[...].astype(F32)

    def masks(b, carry):
        s = scol[b]
        r = rcol[b]
        lane = iota((128, 128), 1)
        rows = pl.ds(pl.multiple_of(b * 128, 128), 128)
        for t in range(5):
            if t < 2:
                m = s == lane + t * 128
            elif t == 2:
                m = ((s == lane + 256) & (lane < 64)) | (r == lane - 64)
            else:
                m = r == lane + (t * 128 - NODES)
            apre[rows, t * 128 : (t + 1) * 128] = hot(m)
        for t in range(4):
            apost[rows, t * 128 : (t + 1) * 128] = hot(s == lane + (NODES + t * 128))
        f = s - (NODES + 8 * HCAP)
        f = jnp.where(
            f >= 0,
            lax.shift_left(lax.bitwise_and(lax.shift_right_arithmetic(f, 1), 7), 5)
            + lax.shift_left(lax.shift_right_arithmetic(f, 4), 1)
            + lax.bitwise_and(f, 1),
            -1,
        )
        for t in range(2):
            apost[rows, 512 + t * 128 : 512 + (t + 1) * 128] = hot(f == lane + t * 128)
        lanes = pl.ds(pl.multiple_of(b * 128, 128), 128)
        rmask[:, lanes] = hot(iota((NODES, 128), 0) == mrow_ref[:, lanes])
        return carry

    lax.fori_loop(0, MEDGES // 128, masks, 0)

    centre("wpo")
    w_copies["wpe"].wait()
    wcat[...] = jnp.zeros_like(wcat)
    wcat[0:4, 0:L] = wmf_ref[...].astype(F32)
    wcat[:, L : 2 * L] = dot(wcat[:, 0:L].astype(BF16), weight("wpe"))

    def landed(k):
        return pltpu.make_async_remote_copy(
            src_ref=eout.at[k],
            dst_ref=ein.at[k],
            send_sem=es_sem.at[k],
            recv_sem=er_sem.at[k],
            device_id=near_id(CODES[0]),
            device_id_type=MESH,
        )

    def arrive(g, carry):
        for i in range(2):
            landed(2 * g + i).wait_recv()
        mbuf[...] += encode(ein[pl.ds(2 * g, 2)], 2)
        return carry

    lax.fori_loop(0, 4, arrive, 0)

    w_copies["wni"].wait()
    w_copies["wno"].wait()
    h = silu(dot(mbuf[...].astype(BF16), weight("wni"))).astype(BF16)
    latent = normalize(dot(h, weight("wno"))).astype(BF16)
    lat_buf[...] = latent
    w_copies["wps"].wait()
    own = dot(latent, weight("wps")).astype(BF16)
    tpre[0:NODES, :] = own
    near_out[...] = dot(gsend[0:512, :], own).astype(BF16).reshape(8, HCAP, L)

    def near_copy(e):
        return pltpu.make_async_remote_copy(
            src_ref=near_out.at[e],
            dst_ref=tpost.at[7 - e],
            send_sem=ns_sem.at[e],
            recv_sem=nr_sem.at[e],
            device_id=near_id(e if e < 4 else e + 1),
            device_id_type=MESH,
        )

    for e in (0, 2, 5, 7, 3, 4, 1, 6):
        near_copy(e).start()

    a_out[...] = dot(gsend[512:768, :], own).astype(BF16).reshape(16, 16, L)

    def a_copy(i):
        other, device = a_peer(i)
        return pltpu.make_async_remote_copy(
            src_ref=a_out.at[other],
            dst_ref=a_in.at[zx],
            send_sem=as_sem.at[i],
            recv_sem=ar_sem.at[i],
            device_id=device,
            device_id_type=MESH,
        )

    def a_start(i, carry):
        a_copy(i).start()
        return carry

    lax.fori_loop(1, 16, a_start, 0)
    a_in[zx] = a_out[zx]

    w_copies["wpr"].wait()
    tpre[NODES : 2 * NODES, :] = dot(latent, weight("wpr")).astype(BF16)

    def ahead(b, carry):
        rows = pl.ds(pl.multiple_of(b * BLK, BLK), BLK)
        embed = dot_tn(featp[:, rows].astype(BF16), wcat[...].astype(BF16))
        obuf[rows, :] = embed[:, 0:L].astype(BF16)
        pre[rows, :] = dot(apre[rows, :], tpre[...]) + embed[:, L : 2 * L]
        return carry

    lax.fori_loop(0, NBLK // 2, ahead, 0)

    def a_wait(i, carry):
        a_copy(i).wait_recv()
        return carry

    lax.fori_loop(1, 16, a_wait, 0)
    j = iota((256, 256), 0)
    source = (
        lax.shift_left(lax.bitwise_and(lax.shift_right_logical(j, 1), 15), 4)
        + lax.shift_left(lax.shift_right_logical(j, 5), 1)
        + lax.bitwise_and(j, 1)
    )
    turn = hot(iota((256, 256), 1) == source)
    b_out[...] = dot(turn, a_in[...].reshape(256, L)).astype(BF16).reshape(8, 32, L)

    def b_copy(i):
        other, device = b_peer(i)
        return pltpu.make_async_remote_copy(
            src_ref=b_out.at[other],
            dst_ref=tpost.at[8 + lax.div(spot, 2), pl.ds(pl.multiple_of(lax.rem(spot, 2) * 32, 32), 32)],
            send_sem=bs_sem.at[i],
            recv_sem=br_sem.at[i],
            device_id=device,
            device_id_type=MESH,
        )

    def b_start(i, carry):
        b_copy(i).start()
        return carry

    lax.fori_loop(1, 8, b_start, 0)
    tpost[8 + lax.div(spot, 2), pl.ds(pl.multiple_of(lax.rem(spot, 2) * 32, 32), 32), :] = b_out[spot]

    lax.fori_loop(NBLK // 2, NBLK, ahead, 0)

    for e in range(8):
        near_copy(e).wait_recv()

    def b_wait(i, carry):
        b_copy(i).wait_recv()
        return carry

    lax.fori_loop(1, 8, b_wait, 0)

    mbuf[...] = jnp.zeros_like(mbuf)

    def out_copy(b):
        rows = pl.ds(pl.multiple_of(b * BLK, BLK), BLK)
        return pltpu.make_async_copy(obuf.at[rows], edge_out.at[rows], o_sem.at[b])

    def process(b, carry):
        rows = pl.ds(pl.multiple_of(b * BLK, BLK), BLK)
        v = pre[rows, :] + dot(apost[rows, :], tpost[...].reshape(768, L))
        h = silu(v).astype(BF16)
        out = (obuf[rows, :].astype(F32) + scaled(dot(h, weight("wpo")))).astype(BF16)
        obuf[rows, :] = out
        out_copy(b).start()
        mbuf[...] += dot(rmask[:, rows], out)
        return carry

    lax.fori_loop(0, NBLK, process, 0)

    w_copies["wus"].wait()
    w_copies["wua"].wait()
    w_copies["wuo"].wait()
    h = dot(lat_buf[...], weight("wus")) + dot(mbuf[...].astype(BF16), weight("wua"))
    h = silu(h).astype(BF16)
    mesh_out[...] = (lat_buf[...].astype(F32) + normalize(dot(h, weight("wuo")))).astype(BF16)

    for k in range(8):
        edge_copy(k).wait_send()
        near_copy(k).wait_send()

    def a_sent(i, carry):
        a_copy(i).wait_send()
        return carry

    def b_sent(i, carry):
        b_copy(i).wait_send()
        return carry

    def o_sent(b, carry):
        out_copy(b).wait()
        return carry

    lax.fori_loop(1, 16, a_sent, 0)
    lax.fori_loop(1, 8, b_sent, 0)
    lax.fori_loop(0, NBLK, o_sent, 0)


def on_device(
    grid_in, g2m_senders, g2m_dest, g2m_receivers, g2m_feat, halo_near, halo_far, mesh_senders,
    mesh_receivers, mesh_feat, w_grid_in, w_grid_out, w_edge_latent, w_edge_feat, w_edge_out, w_node_in,
    w_node_out, w_mesh_feat, w_proc_edge, w_proc_send, w_proc_recv, w_proc_out, w_upd_self, w_upd_sum,
    w_upd_out,
):
    idx = jnp.concatenate(
        [
            g2m_senders, halo_near.reshape(-1), halo_far.reshape(-1), mesh_senders, mesh_receivers,
            jnp.zeros((128 * 128 - 52 * 128,), I32),
        ]
    ).reshape(128, 128)
    vm = pl.BlockSpec(memory_space=pltpu.VMEM)
    hb = pl.BlockSpec(memory_space=pl.ANY)
    dma = pltpu.SemaphoreType.DMA
    return pl.pallas_call(
        kernel,
        out_shape=(
            jax.ShapeDtypeStruct((NODES, L), BF16),
            jax.ShapeDtypeStruct((MEDGES, L), BF16),
        ),
        in_specs=[hb, vm, vm, vm, vm, vm, vm, hb, vm, vm] + [hb] * 12,
        out_specs=(vm, hb),
        scratch_shapes=[
            pltpu.VMEM((GRID_N, CIN), BF16),
            pltpu.VMEM((EDGES, 256), BF16),
            pltpu.VMEM((CIN, L), BF16),
            pltpu.VMEM((256, L), F32),
            pltpu.VMEM((256, L), BF16),
            pltpu.VMEM((12, L, L), BF16),
            pltpu.VMEM((16, EDGES), F32),
            pltpu.VMEM((16, L), F32),
            pltpu.VMEM((16, MEDGES), F32),
            pltpu.VMEM((16, 2 * L), F32),
            pltpu.VMEM((8, SLOT, 256), BF16),
            pltpu.VMEM((9, SLOT, 256), BF16),
            pltpu.VMEM((MEDGES // 128, 128, 128), I32),
            pltpu.VMEM((MEDGES // 128, 128, 128), I32),
            pltpu.VMEM((MEDGES, 2 * NODES), BF16),
            pltpu.VMEM((MEDGES, 768), BF16),
            pltpu.VMEM((NODES, MEDGES), BF16),
            pltpu.VMEM((768, NODES), BF16),
            pltpu.VMEM((2 * NODES, L), BF16),
            pltpu.VMEM((12, 64, L), BF16),
            pltpu.VMEM((8, HCAP, L), BF16),
            pltpu.VMEM((16, 16, L), BF16),
            pltpu.VMEM((16, 16, L), BF16),
            pltpu.VMEM((8, 32, L), BF16),
            pltpu.VMEM((MEDGES, L), F32),
            pltpu.VMEM((MEDGES, L), BF16),
            pltpu.VMEM((NODES, L), BF16),
            pltpu.VMEM((NODES, L), F32),
            dma((2,)),
            dma((12,)),
            dma((8,)),
            dma((8,)),
            dma((8,)),
            dma((8,)),
            dma((16,)),
            dma((16,)),
            dma((8,)),
            dma((8,)),
            dma((NBLK,)),
        ],
        compiler_params=pltpu.CompilerParams(
            collective_id=0, has_side_effects=True, vmem_limit_bytes=60 * 1024 * 1024
        ),
        cost_estimate=pl.CostEstimate(flops=15_000_000_000, bytes_accessed=12_000_000, transcendentals=4_000_000),
    )(
        grid_in, idx, g2m_dest.reshape(1, EDGES), g2m_receivers.reshape(1, EDGES), g2m_feat,
        mesh_receivers.reshape(1, MEDGES), mesh_feat, w_grid_in, w_edge_feat, w_mesh_feat,
        w_grid_out, w_edge_latent, w_edge_out, w_node_in, w_node_out, w_proc_edge, w_proc_send, w_proc_recv,
        w_proc_out, w_upd_self, w_upd_sum, w_upd_out,
    )


def solution(mesh):
    both = ("lat", "lon")
    rows, flat, cube = P(both, None), P(both), P(both, None, None)
    return jax.shard_map(
        on_device,
        mesh=mesh,
        in_specs=(rows, flat, rows, flat, P(None, both), cube, cube, flat, flat, P(None, both)) + (P(),) * 15,
        out_specs=(rows, rows),
        check_vma=False,
    )
```

```python
import functools

import jax
import jax.numpy as jnp
from jax import lax
from jax.experimental import pallas as pl
from jax.experimental.pallas import tpu as pltpu
from jax.sharding import PartitionSpec as P

F32 = jnp.float32
BF16 = jnp.bfloat16
I32 = jnp.int32
MESH = pl.DeviceIdType.MESH

N_LAT, N_LON = 32, 4
L = 512
CIN = 227
GRID_N = 1024
EDGES = 768
NODES = 320
MEDGES = 2560
CAP = 192
HCAP = 64
SLOT = CAP + 16
BLK = 256
NBLK = MEDGES // BLK

CODES = (1, 7, 3, 5, 0, 2, 6, 8)
SEND_ORDER = (4, 5, 6, 7, 2, 3, 0, 1)

COL_SEND = 0
COL_NEAR = 6
COL_FAR = 10
COL_MS = 12
COL_MR = 32

W_NAMES = (
    "wgo", "wel", "weo", "wni", "wno", "wpe", "wps", "wpr", "wpo", "wus", "wua", "wuo",
)


def dot(a, b):
    return jnp.dot(a, b, preferred_element_type=F32)


def dot_tn(a, b):
    return lax.dot_general(a, b, (((0,), (0,)), ((), ())), preferred_element_type=F32)


def dot_nt(a, b):
    return lax.dot_general(a, b, (((1,), (1,)), ((), ())), preferred_element_type=F32)


def silu(v):
    h = 0.5 * v
    return h + h * jnp.tanh(h)


def scaled(v):
    return v * lax.rsqrt(jnp.mean(v * v, axis=-1, keepdims=True) + 1e-05)


def normalize(v):
    c = v - jnp.mean(v, axis=-1, keepdims=True)
    return c * lax.rsqrt(jnp.mean(c * c, axis=-1, keepdims=True) + 1e-05)


def iota(shape, dim):
    return lax.broadcasted_iota(I32, shape, dim)


def hot(mask):
    return jnp.where(mask, 1.0, 0.0).astype(BF16)


def kernel(
    grid_hbm, send_ref, dest_ref, recv_ref, gfeat_ref, near_ref, far_ref, msend_ref, mrecv_ref, mfeat_ref,
    wgi_hbm, wef_ref, wmf_ref,
    wgo_h, wel_h, weo_h, wni_h, wno_h, wpe_h, wps_h, wpr_h, wpo_h, wus_h, wua_h, wuo_h,
    mesh_out, edge_out,
    idx, mrow_ref, graw, gsel, wraw, wpad32, wgi, wts, aux, wefp, featp, wcat,
    eout, ein, scol, rcol, apre, apost, rmask, gsend,
    tpre, tpost, near_out, a_out, a_in, b_out, pre, obuf, lat_buf, mbuf,
    in_sem, w_sem, es_sem, er_sem, ns_sem, nr_sem, as_sem, ar_sem, bs_sem, br_sem, o_sem,
):
    lat = lax.axis_index("lat")
    lon = lax.axis_index("lon")
    zx = lax.div(lat, 2)
    core = lax.rem(lat, 2)
    spot = core * 4 + lon

    def near_id(code):
        return (
            lax.rem(lat + (code // 3 - 1) + N_LAT, N_LAT),
            lax.rem(lon + (code % 3 - 1) + N_LON, N_LON),
        )

    def a_peer(i):
        other = lax.rem(zx + i, 16)
        return other, (other * 2 + core, lon)

    def b_peer(i):
        other = lax.rem(spot + i, 8)
        return other, (zx * 2 + lax.div(other, 4), lax.rem(other, 4))

    barrier = pltpu.get_barrier_semaphore()
    for code in CODES:
        pl.semaphore_signal(barrier, inc=1, device_id=near_id(code), device_id_type=MESH)

    def greet_a(i, carry):
        pl.semaphore_signal(barrier, inc=1, device_id=a_peer(i)[1], device_id_type=MESH)
        return carry

    def greet_b(i, carry):
        pl.semaphore_signal(barrier, inc=1, device_id=b_peer(i)[1], device_id_type=MESH)
        return carry

    lax.fori_loop(1, 16, greet_a, 0)
    lax.fori_loop(1, 8, greet_b, 0)

    g_copy = pltpu.make_async_copy(grid_hbm, graw, in_sem.at[0])
    g_copy.start()
    wi_copy = pltpu.make_async_copy(wgi_hbm, wraw, in_sem.at[1])
    wi_copy.start()
    w_copies = {}
    for k, (name, ref) in enumerate(
        zip(W_NAMES, (wgo_h, wel_h, weo_h, wni_h, wno_h, wpe_h, wps_h, wpr_h, wpo_h, wus_h, wua_h, wuo_h))
    ):
        w_copies[name] = pltpu.make_async_copy(ref, wts.at[k], w_sem.at[k])
        w_copies[name].start()

    def weight(name):
        return wts[W_NAMES.index(name)]

    codes = dest_ref[...]
    marks = jnp.where(iota((16, EDGES), 0) == codes, 1.0, 0.0)
    below = hot(iota((EDGES, EDGES), 0) < iota((EDGES, EDGES), 1))
    earlier = dot(marks.astype(BF16), below)
    rank = jnp.sum(earlier * marks, axis=0, keepdims=True).astype(I32)
    place = codes * CAP + rank

    name_row = recv_ref[...].reshape(1, EDGES) + 1
    aux[...] = jnp.zeros_like(aux)
    aux[0:1, :] = lax.shift_right_logical(name_row, 4).astype(F32)
    aux[1:2, :] = lax.bitwise_and(name_row, 15).astype(F32)
    aux[4:8, :] = gfeat_ref[...].astype(F32)
    aux_rows = aux[...].astype(BF16)

    idx[COL_SEND : COL_SEND + 6, :] = send_ref[...].reshape(6, 128)
    for e in range(8):
        idx[COL_NEAR + e // 2 : COL_NEAR + e // 2 + 1, e % 2 * 64 : e % 2 * 64 + 64] = near_ref[e : e + 1, :]
    idx[COL_FAR : COL_FAR + 2, :] = far_ref[...]
    idx[COL_MS : COL_MS + 20, :] = msend_ref[...].reshape(20, 128)
    idx[COL_MR : COL_MR + 20, :] = mrecv_ref[...].reshape(20, 128)
    idx[COL_MR + 20 :, :] = jnp.zeros((128 - COL_MR - 20, 128), I32)
    mrow_ref[...] = mrecv_ref[...].reshape(1, MEDGES)
    idx_t = jnp.transpose(idx[...])

    g_copy.wait()
    gsel[:, 128:256] = jnp.zeros((EDGES, 128), BF16)
    for b in range(EDGES // 128):
        pick = hot(idx_t[:, COL_SEND + b : COL_SEND + b + 1] == iota((128, GRID_N), 1))
        gsel[b * 128 : (b + 1) * 128, 0:CIN] = dot_nt(pick, graw[...]).astype(BF16)

    def pack(code, target, k):
        choose = hot(iota((CAP, EDGES), 0) + code * CAP == place)
        target[k, 0:CAP, :] = dot(choose, gsel[...]).astype(BF16)
        target[k, CAP:SLOT, :] = jnp.zeros((16, 256), BF16)
        target[k, CAP:SLOT, 0:CAP] = dot_nt(aux_rows, choose).astype(BF16)

    def edge_copy(k):
        return pltpu.make_async_remote_copy(
            src_ref=eout.at[k],
            dst_ref=ein.at[k],
            send_sem=es_sem.at[k],
            recv_sem=er_sem.at[k],
            device_id=near_id(CODES[k]),
            device_id_type=MESH,
        )

    for n, k in enumerate(SEND_ORDER):
        pack(CODES[k], eout, k)
        if n == 0:
            pl.semaphore_wait(barrier, 8 + 15 + 7)
        edge_copy(k).start()
    pack(4, ein, 8)

    wi_copy.wait()
    wpad32[224:256, :] = jnp.zeros((32, L), F32)
    wpad32[0:CIN, :] = wraw[...].astype(F32)
    wgi[...] = wpad32[...].astype(BF16)
    wefp[...] = jnp.zeros_like(wefp)
    wefp[4:8, :] = wef_ref[...].astype(F32)

    def centre(name):
        w_copies[name].wait()
        w = weight(name).astype(F32)
        wts[W_NAMES.index(name)] = (w - jnp.mean(w, axis=-1, keepdims=True)).astype(BF16)

    centre("wgo")
    w_copies["wel"].wait()
    centre("weo")

    def encode(slots, count):
        x = slots[:, 0:CAP, :].reshape(count * CAP, 256)
        h = silu(dot(x, wgi[...])).astype(BF16)
        latent = scaled(dot(h, weight("wgo"))).astype(BF16)
        wf = wefp[...].astype(BF16)
        tails = [slots[i, CAP:SLOT, :][:, 0:CAP] for i in range(count)]
        feat_part = jnp.concatenate([dot_tn(t, wf) for t in tails], axis=0) if count > 1 else dot_tn(tails[0], wf)
        h = silu(dot(latent, weight("wel")) + feat_part).astype(BF16)
        message = scaled(dot(h, weight("weo"))).astype(BF16)
        total = None
        for i in range(count):
            t = tails[i].astype(F32)
            node = (t[0:1, :] * 16.0 + t[1:2, :] - 1.0).astype(I32)
            part = dot(hot(iota((NODES, CAP), 0) == node), message[i * CAP : (i + 1) * CAP])
            total = part if total is None else total + part
        return total

    mbuf[...] = encode(ein[8:9], 1)

    for b in range(MEDGES // 128):
        scol[b] = jnp.broadcast_to(idx_t[:, COL_MS + b : COL_MS + b + 1], (128, 128))
        rcol[b] = jnp.broadcast_to(idx_t[:, COL_MR + b : COL_MR + b + 1], (128, 128))
    def node_hot(c):
        return hot(idx_t[:, c : c + 1] == iota((128, NODES), 1))

    for b in range(4):
        gsend[b * 128 : (b + 1) * 128, :] = node_hot(COL_NEAR + b)
    j = iota((256, 256), 0)
    source = (
        lax.shift_left(lax.bitwise_and(lax.shift_right_logical(j, 3), 1), 7)
        + lax.shift_left(lax.shift_right_logical(j, 4), 3)
        + lax.bitwise_and(j, 7)
    )
    turn = hot(iota((256, 256), 1) == source)
    far_hot = jnp.concatenate([node_hot(COL_FAR), node_hot(COL_FAR + 1)], axis=0)
    gsend[512:768, :] = dot(turn, far_hot).astype(BF16)

    featp[...] = jnp.zeros_like(featp)
    featp[0:4, :] = mfeat_ref[...].astype(F32)

    def masks(b, carry):
        s = scol[b]
        r = rcol[b]
        lane = iota((128, 128), 1)
        rows = pl.ds(pl.multiple_of(b * 128, 128), 128)
        for t in range(5):
            if t < 2:
                m = s == lane + t * 128
            elif t == 2:
                m = ((s == lane + 256) & (lane < 64)) | (r == lane - 64)
            else:
                m = r == lane + (t * 128 - NODES)
            apre[rows, t * 128 : (t + 1) * 128] = hot(m)
        for t in range(4):
            apost[rows, t * 128 : (t + 1) * 128] = hot(s == lane + (NODES + t * 128))
        f = s - (NODES + 8 * HCAP)
        f = jnp.where(
            f >= 0,
            lax.shift_left(lax.bitwise_and(lax.shift_right_arithmetic(f, 1), 7), 5)
            + lax.shift_left(lax.shift_right_arithmetic(f, 4), 1)
            + lax.bitwise_and(f, 1),
            -1,
        )
        for t in range(2):
            apost[rows, 512 + t * 128 : 512 + (t + 1) * 128] = hot(f == lane + t * 128)
        lanes = pl.ds(pl.multiple_of(b * 128, 128), 128)
        rmask[:, lanes] = hot(iota((NODES, 128), 0) == mrow_ref[:, lanes])
        return carry

    lax.fori_loop(0, MEDGES // 128, masks, 0)

    centre("wpo")
    w_copies["wpe"].wait()
    wcat[...] = jnp.zeros_like(wcat)
    wcat[0:4, 0:L] = wmf_ref[...].astype(F32)
    wcat[:, L : 2 * L] = dot(wcat[:, 0:L].astype(BF16), weight("wpe"))

    def landed(k):
        return pltpu.make_async_remote_copy(
            src_ref=eout.at[k],
            dst_ref=ein.at[k],
            send_sem=es_sem.at[k],
            recv_sem=er_sem.at[k],
            device_id=near_id(CODES[0]),
            device_id_type=MESH,
        )

    def arrive(g, carry):
        for i in range(2):
            landed(2 * g + i).wait_recv()
        mbuf[...] += encode(ein[pl.ds(2 * g, 2)], 2)
        return carry

    lax.fori_loop(0, 4, arrive, 0)

    w_copies["wni"].wait()
    w_copies["wno"].wait()
    h = silu(dot(mbuf[...].astype(BF16), weight("wni"))).astype(BF16)
    latent = normalize(dot(h, weight("wno"))).astype(BF16)
    lat_buf[...] = latent
    w_copies["wps"].wait()
    own = dot(latent, weight("wps")).astype(BF16)
    tpre[0:NODES, :] = own
    near_out[...] = dot(gsend[0:512, :], own).astype(BF16).reshape(8, HCAP, L)

    def near_copy(e):
        return pltpu.make_async_remote_copy(
            src_ref=near_out.at[e],
            dst_ref=tpost.at[7 - e],
            send_sem=ns_sem.at[e],
            recv_sem=nr_sem.at[e],
            device_id=near_id(e if e < 4 else e + 1),
            device_id_type=MESH,
        )

    for e in (0, 2, 5, 7, 3, 4, 1, 6):
        near_copy(e).start()

    a_out[...] = dot(gsend[512:768, :], own).astype(BF16).reshape(16, 16, L)

    def a_copy(i):
        other, device = a_peer(i)
        return pltpu.make_async_remote_copy(
            src_ref=a_out.at[other],
            dst_ref=a_in.at[zx],
            send_sem=as_sem.at[i],
            recv_sem=ar_sem.at[i],
            device_id=device,
            device_id_type=MESH,
        )

    def a_start(i, carry):
        a_copy(i).start()
        return carry

    lax.fori_loop(1, 16, a_start, 0)
    a_in[zx] = a_out[zx]

    w_copies["wpr"].wait()
    tpre[NODES : 2 * NODES, :] = dot(latent, weight("wpr")).astype(BF16)

    def ahead(b, carry):
        rows = pl.ds(pl.multiple_of(b * BLK, BLK), BLK)
        embed = dot_tn(featp[:, rows].astype(BF16), wcat[...].astype(BF16))
        obuf[rows, :] = embed[:, 0:L].astype(BF16)
        pre[rows, :] = dot(apre[rows, :], tpre[...]) + embed[:, L : 2 * L]
        return carry

    lax.fori_loop(0, NBLK // 2, ahead, 0)

    def a_wait(i, carry):
        a_copy(i).wait_recv()
        return carry

    lax.fori_loop(1, 16, a_wait, 0)
    j = iota((256, 256), 0)
    source = (
        lax.shift_left(lax.bitwise_and(lax.shift_right_logical(j, 1), 15), 4)
        + lax.shift_left(lax.bitwise_and(j, 1), 3)
        + lax.shift_right_logical(j, 5)
    )
    turn = hot(iota((256, 256), 1) == source)
    b_out[...] = dot(turn, a_in[...].reshape(256, L)).astype(BF16).reshape(8, 32, L)

    def b_copy(i):
        other, device = b_peer(i)
        return pltpu.make_async_remote_copy(
            src_ref=b_out.at[other],
            dst_ref=tpost.at[8 + lax.div(spot, 2), pl.ds(pl.multiple_of(lax.rem(spot, 2) * 32, 32), 32)],
            send_sem=bs_sem.at[i],
            recv_sem=br_sem.at[i],
            device_id=device,
            device_id_type=MESH,
        )

    def b_start(i, carry):
        b_copy(i).start()
        return carry

    lax.fori_loop(1, 8, b_start, 0)
    tpost[8 + lax.div(spot, 2), pl.ds(pl.multiple_of(lax.rem(spot, 2) * 32, 32), 32), :] = b_out[spot]

    lax.fori_loop(NBLK // 2, NBLK, ahead, 0)

    for e in range(8):
        near_copy(e).wait_recv()

    def b_wait(i, carry):
        b_copy(i).wait_recv()
        return carry

    lax.fori_loop(1, 8, b_wait, 0)

    mbuf[...] = jnp.zeros_like(mbuf)

    def out_copy(b):
        rows = pl.ds(pl.multiple_of(b * BLK, BLK), BLK)
        return pltpu.make_async_copy(obuf.at[rows], edge_out.at[rows], o_sem.at[b])

    def process(b, carry):
        rows = pl.ds(pl.multiple_of(b * BLK, BLK), BLK)
        v = pre[rows, :] + dot(apost[rows, :], tpost[...].reshape(768, L))
        h = silu(v).astype(BF16)
        out = (obuf[rows, :].astype(F32) + scaled(dot(h, weight("wpo")))).astype(BF16)
        obuf[rows, :] = out
        out_copy(b).start()
        mbuf[...] += dot(rmask[:, rows], out)
        return carry

    lax.fori_loop(0, NBLK, process, 0)

    w_copies["wus"].wait()
    w_copies["wua"].wait()
    w_copies["wuo"].wait()
    h = dot(lat_buf[...], weight("wus")) + dot(mbuf[...].astype(BF16), weight("wua"))
    h = silu(h).astype(BF16)
    mesh_out[...] = (lat_buf[...].astype(F32) + normalize(dot(h, weight("wuo")))).astype(BF16)

    for k in range(8):
        edge_copy(k).wait_send()
        near_copy(k).wait_send()

    def a_sent(i, carry):
        a_copy(i).wait_send()
        return carry

    def b_sent(i, carry):
        b_copy(i).wait_send()
        return carry

    def o_sent(b, carry):
        out_copy(b).wait()
        return carry

    lax.fori_loop(1, 16, a_sent, 0)
    lax.fori_loop(1, 8, b_sent, 0)
    lax.fori_loop(0, NBLK, o_sent, 0)


def on_device(
    grid_in, g2m_senders, g2m_dest, g2m_receivers, g2m_feat, halo_near, halo_far, mesh_senders,
    mesh_receivers, mesh_feat, w_grid_in, w_grid_out, w_edge_latent, w_edge_feat, w_edge_out, w_node_in,
    w_node_out, w_mesh_feat, w_proc_edge, w_proc_send, w_proc_recv, w_proc_out, w_upd_self, w_upd_sum,
    w_upd_out,
):
    vm = pl.BlockSpec(memory_space=pltpu.VMEM)
    hb = pl.BlockSpec(memory_space=pl.ANY)
    dma = pltpu.SemaphoreType.DMA
    return pl.pallas_call(
        kernel,
        out_shape=(
            jax.ShapeDtypeStruct((NODES, L), BF16),
            jax.ShapeDtypeStruct((MEDGES, L), BF16),
        ),
        in_specs=[hb, vm, vm, vm, vm, vm, vm, vm, vm, vm, hb, vm, vm] + [hb] * 12,
        out_specs=(vm, hb),
        scratch_shapes=[
            pltpu.VMEM((128, 128), I32),
            pltpu.VMEM((1, MEDGES), I32),
            pltpu.VMEM((CIN, GRID_N), BF16),
            pltpu.VMEM((EDGES, 256), BF16),
            pltpu.VMEM((CIN, L), BF16),
            pltpu.VMEM((256, L), F32),
            pltpu.VMEM((256, L), BF16),
            pltpu.VMEM((12, L, L), BF16),
            pltpu.VMEM((16, EDGES), F32),
            pltpu.VMEM((16, L), F32),
            pltpu.VMEM((16, MEDGES), F32),
            pltpu.VMEM((16, 2 * L), F32),
            pltpu.VMEM((8, SLOT, 256), BF16),
            pltpu.VMEM((9, SLOT, 256), BF16),
            pltpu.VMEM((MEDGES // 128, 128, 128), I32),
            pltpu.VMEM((MEDGES // 128, 128, 128), I32),
            pltpu.VMEM((MEDGES, 2 * NODES), BF16),
            pltpu.VMEM((MEDGES, 768), BF16),
            pltpu.VMEM((NODES, MEDGES), BF16),
            pltpu.VMEM((768, NODES), BF16),
            pltpu.VMEM((2 * NODES, L), BF16),
            pltpu.VMEM((12, 64, L), BF16),
            pltpu.VMEM((8, HCAP, L), BF16),
            pltpu.VMEM((16, 16, L), BF16),
            pltpu.VMEM((16, 16, L), BF16),
            pltpu.VMEM((8, 32, L), BF16),
            pltpu.VMEM((MEDGES, L), F32),
            pltpu.VMEM((MEDGES, L), BF16),
            pltpu.VMEM((NODES, L), BF16),
            pltpu.VMEM((NODES, L), F32),
            dma((2,)),
            dma((12,)),
            dma((8,)),
            dma((8,)),
            dma((8,)),
            dma((8,)),
            dma((16,)),
            dma((16,)),
            dma((8,)),
            dma((8,)),
            dma((NBLK,)),
        ],
        compiler_params=pltpu.CompilerParams(
            collective_id=0, has_side_effects=True, vmem_limit_bytes=60 * 1024 * 1024
        ),
        cost_estimate=pl.CostEstimate(flops=15_000_000_000, bytes_accessed=12_000_000, transcendentals=4_000_000),
    )(
        grid_in.T, g2m_senders, g2m_dest.reshape(1, EDGES), g2m_receivers, g2m_feat,
        halo_near.reshape(8, HCAP), halo_far.reshape(128, 2).T, mesh_senders, mesh_receivers, mesh_feat, w_grid_in, w_edge_feat, w_mesh_feat,
        w_grid_out, w_edge_latent, w_edge_out, w_node_in, w_node_out, w_proc_edge, w_proc_send, w_proc_recv,
        w_proc_out, w_upd_self, w_upd_sum, w_upd_out,
    )


def solution(mesh):
    both = ("lat", "lon")
    rows, flat, cube = P(both, None), P(both), P(both, None, None)
    return jax.shard_map(
        on_device,
        mesh=mesh,
        in_specs=(rows, flat, rows, flat, P(None, both), cube, cube, flat, flat, P(None, both)) + (P(),) * 15,
        out_specs=(rows, rows),
        check_vma=False,
    )
```

```python
import functools

import jax
import jax.numpy as jnp
from jax import lax
from jax.experimental import pallas as pl
from jax.experimental.pallas import tpu as pltpu
from jax.sharding import PartitionSpec as P

F32 = jnp.float32
BF16 = jnp.bfloat16
I32 = jnp.int32
MESH = pl.DeviceIdType.MESH

N_LAT, N_LON = 32, 4
L = 512
CIN = 227
GRID_N = 1024
EDGES = 768
NODES = 320
MEDGES = 2560
CAP = 192
HCAP = 64
SLOT = CAP + 16
BLK = 256
NBLK = MEDGES // BLK
AHEAD = 5

CODES = (1, 7, 3, 5, 0, 2, 6, 8)
SEND_ORDER = (4, 5, 6, 7, 2, 3, 0, 1)

COL_SEND = 0
COL_NEAR = 6
COL_FAR = 10
COL_MS = 12
COL_MR = 32

W_NAMES = (
    "wgo", "wel", "weo", "wni", "wno", "wpe", "wps", "wpr", "wpo", "wus", "wua", "wuo",
)


def dot(a, b):
    return jnp.dot(a, b, preferred_element_type=F32)


def dot_tn(a, b):
    return lax.dot_general(a, b, (((0,), (0,)), ((), ())), preferred_element_type=F32)


def dot_nt(a, b):
    return lax.dot_general(a, b, (((1,), (1,)), ((), ())), preferred_element_type=F32)


def silu(v):
    h = 0.5 * v
    return h + h * jnp.tanh(h)


def scaled(v):
    return v * lax.rsqrt(jnp.mean(v * v, axis=-1, keepdims=True) + 1e-05)


def normalize(v):
    c = v - jnp.mean(v, axis=-1, keepdims=True)
    return c * lax.rsqrt(jnp.mean(c * c, axis=-1, keepdims=True) + 1e-05)


def far_order(kind):
    j = iota((256, 256), 0)
    row = lax.bitwise_and(j, 1)
    if kind == 0:
        return lax.bitwise_and(lax.shift_right_logical(j, 1), 7) * 32 + lax.shift_right_logical(j, 4) * 2 + row
    return lax.bitwise_and(lax.shift_right_logical(j, 1), 15) * 16 + lax.shift_right_logical(j, 5) * 2 + row


def iota(shape, dim):
    return lax.broadcasted_iota(I32, shape, dim)


def hot(mask):
    return jnp.where(mask, 1.0, 0.0).astype(BF16)


def kernel(
    grid_hbm, send_ref, dest_ref, recv_ref, gfeat_ref, near_ref, far_ref, msend_ref, mrecv_ref, mfeat_ref,
    wgi_hbm, wef_ref, wmf_ref,
    wgo_h, wel_h, weo_h, wni_h, wno_h, wpe_h, wps_h, wpr_h, wpo_h, wus_h, wua_h, wuo_h,
    mesh_out, edge_out,
    idx, mrow_ref, graw, gsel, wraw, wpad32, wgi, wts, aux, wefp, featp, wcat,
    eout, ein, scol, rcol, apre, apost, rmask, gsend,
    tpre, tnear, tfar, near_out, a1_out, a1_in, b1_out, b1_in, b2_out, b2_in, a2_out, a2_in, hbuf,
    pre, obuf, lat_buf, mbuf,
    in_sem, w_sem, es_sem, er_sem, ns_sem, nr_sem, a1s, a1r, b1s, b1r, b2s, b2r, a2s, a2r, o_sem,
):
    lat = lax.axis_index("lat")
    lon = lax.axis_index("lon")
    zx = lax.div(lat, 2)
    core = lax.rem(lat, 2)
    spot = core * 4 + lon

    def near_id(code):
        return (
            lax.rem(lat + (code // 3 - 1) + N_LAT, N_LAT),
            lax.rem(lon + (code % 3 - 1) + N_LON, N_LON),
        )

    def a_peer(i):
        other = lax.rem(zx + i, 16)
        return other, (other * 2 + core, lon)

    def b_peer(i):
        other = lax.rem(spot + i, 8)
        return other, (zx * 2 + lax.div(other, 4), lax.rem(other, 4))

    barrier = pltpu.get_barrier_semaphore()
    for code in CODES:
        pl.semaphore_signal(barrier, inc=1, device_id=near_id(code), device_id_type=MESH)

    def greet_a(i, carry):
        pl.semaphore_signal(barrier, inc=1, device_id=a_peer(i)[1], device_id_type=MESH)
        return carry

    def greet_b(i, carry):
        pl.semaphore_signal(barrier, inc=1, device_id=b_peer(i)[1], device_id_type=MESH)
        return carry

    lax.fori_loop(1, 16, greet_a, 0)
    lax.fori_loop(1, 8, greet_b, 0)

    g_copy = pltpu.make_async_copy(grid_hbm, graw, in_sem.at[0])
    g_copy.start()
    wi_copy = pltpu.make_async_copy(wgi_hbm, wraw, in_sem.at[1])
    wi_copy.start()
    w_copies = {}
    for k, (name, ref) in enumerate(
        zip(W_NAMES, (wgo_h, wel_h, weo_h, wni_h, wno_h, wpe_h, wps_h, wpr_h, wpo_h, wus_h, wua_h, wuo_h))
    ):
        w_copies[name] = pltpu.make_async_copy(ref, wts.at[k], w_sem.at[k])
        w_copies[name].start()

    def weight(name):
        return wts[W_NAMES.index(name)]

    codes = dest_ref[...]
    marks = jnp.where(iota((16, EDGES), 0) == codes, 1.0, 0.0)
    below = hot(iota((EDGES, EDGES), 0) < iota((EDGES, EDGES), 1))
    earlier = dot(marks.astype(BF16), below)
    rank = jnp.sum(earlier * marks, axis=0, keepdims=True).astype(I32)
    place = codes * CAP + rank

    name_row = recv_ref[...].reshape(1, EDGES) + 1
    aux[...] = jnp.zeros_like(aux)
    aux[0:1, :] = lax.shift_right_logical(name_row, 4).astype(F32)
    aux[1:2, :] = lax.bitwise_and(name_row, 15).astype(F32)
    aux[4:8, :] = gfeat_ref[...].astype(F32)
    aux_rows = aux[...].astype(BF16)

    idx[COL_SEND : COL_SEND + 6, :] = send_ref[...].reshape(6, 128)
    for e in range(8):
        idx[COL_NEAR + e // 2 : COL_NEAR + e // 2 + 1, e % 2 * 64 : e % 2 * 64 + 64] = near_ref[e : e + 1, :]
    idx[COL_FAR : COL_FAR + 2, :] = far_ref[...]
    idx[COL_MS : COL_MS + 20, :] = msend_ref[...].reshape(20, 128)
    idx[COL_MR : COL_MR + 20, :] = mrecv_ref[...].reshape(20, 128)
    idx[COL_MR + 20 :, :] = jnp.zeros((128 - COL_MR - 20, 128), I32)
    mrow_ref[...] = mrecv_ref[...].reshape(1, MEDGES)
    idx_t = jnp.transpose(idx[...])

    g_copy.wait()
    gsel[:, 128:256] = jnp.zeros((EDGES, 128), BF16)
    for b in range(EDGES // 128):
        pick = hot(idx_t[:, COL_SEND + b : COL_SEND + b + 1] == iota((128, GRID_N), 1))
        gsel[b * 128 : (b + 1) * 128, 0:CIN] = dot_nt(pick, graw[...]).astype(BF16)

    def pack(code, target, k):
        choose = hot(iota((CAP, EDGES), 0) + code * CAP == place)
        target[k, 0:CAP, :] = dot(choose, gsel[...]).astype(BF16)
        target[k, CAP:SLOT, :] = jnp.zeros((16, 256), BF16)
        target[k, CAP:SLOT, 0:CAP] = dot_nt(aux_rows, choose).astype(BF16)

    def edge_copy(k):
        return pltpu.make_async_remote_copy(
            src_ref=eout.at[k],
            dst_ref=ein.at[k],
            send_sem=es_sem.at[k],
            recv_sem=er_sem.at[k],
            device_id=near_id(CODES[k]),
            device_id_type=MESH,
        )

    for n, k in enumerate(SEND_ORDER):
        pack(CODES[k], eout, k)
        if n == 0:
            pl.semaphore_wait(barrier, 8 + 15 + 7)
        edge_copy(k).start()
    pack(4, ein, 8)

    wi_copy.wait()
    wpad32[224:256, :] = jnp.zeros((32, L), F32)
    wpad32[0:CIN, :] = wraw[...].astype(F32)
    wgi[...] = wpad32[...].astype(BF16)
    wefp[...] = jnp.zeros_like(wefp)
    wefp[4:8, :] = wef_ref[...].astype(F32)

    def centre(name):
        w_copies[name].wait()
        w = weight(name).astype(F32)
        wts[W_NAMES.index(name)] = (w - jnp.mean(w, axis=-1, keepdims=True)).astype(BF16)

    centre("wgo")
    w_copies["wel"].wait()
    centre("weo")

    def encode(slots, count):
        wf = wefp[...].astype(BF16)
        tails = [slots[i, CAP:SLOT, :][:, 0:CAP] for i in range(count)]
        v = [dot(slots[i, 0:CAP, :], wgi[...]) for i in range(count)]
        v = [dot(silu(u).astype(BF16), weight("wgo")) for u in v]
        v = [dot(scaled(u).astype(BF16), weight("wel")) + dot_tn(t, wf) for u, t in zip(v, tails)]
        v = [dot(silu(u).astype(BF16), weight("weo")) for u in v]
        total = None
        for u, t in zip(v, tails):
            t = t.astype(F32)
            node = (t[0:1, :] * 16.0 + t[1:2, :] - 1.0).astype(I32)
            part = dot(hot(iota((NODES, CAP), 0) == node), scaled(u).astype(BF16))
            total = part if total is None else total + part
        return total

    mbuf[...] = encode(ein[8:9], 1)

    for b in range(MEDGES // 128):
        scol[b] = jnp.broadcast_to(idx_t[:, COL_MS + b : COL_MS + b + 1], (128, 128))
        rcol[b] = jnp.broadcast_to(idx_t[:, COL_MR + b : COL_MR + b + 1], (128, 128))
    def node_hot(c):
        return hot(idx_t[:, c : c + 1] == iota((128, NODES), 1))

    for b in range(4):
        gsend[b * 128 : (b + 1) * 128, :] = node_hot(COL_NEAR + b)
    j = iota((256, 256), 0)
    k = iota((256, 256), 1)
    j_row = lax.bitwise_and(j, 1)
    j_zx = lax.bitwise_and(lax.shift_right_logical(j, 1), 15)
    j_spot = lax.shift_right_logical(j, 5)
    far_hot = jnp.concatenate([node_hot(COL_FAR), node_hot(COL_FAR + 1)], axis=0)
    gsend[512:768, :] = dot(hot(k == j_row * 128 + lax.shift_right_logical(j, 1)), far_hot).astype(BF16)
    gsend[768:1024, :] = dot(hot(k == j_row * 128 + j_zx * 8 + j_spot), far_hot).astype(BF16)

    featp[...] = jnp.zeros_like(featp)
    featp[0:4, :] = mfeat_ref[...].astype(F32)

    def masks(b, carry):
        s = scol[b]
        r = rcol[b]
        lane = iota((128, 128), 1)
        rows = pl.ds(pl.multiple_of(b * 128, 128), 128)
        for t in range(5):
            if t < 2:
                m = s == lane + t * 128
            elif t == 2:
                m = ((s == lane + 256) & (lane < 64)) | (r == lane - 64)
            else:
                m = r == lane + (t * 128 - NODES)
            apre[rows, t * 128 : (t + 1) * 128] = hot(m)
        for t in range(4):
            apost[rows, t * 128 : (t + 1) * 128] = hot(s == lane + (NODES + t * 128))
        f = s - (NODES + 8 * HCAP)
        for t in range(2):
            apost[rows, 512 + t * 128 : 512 + (t + 1) * 128] = hot(f == lane + t * 128)
        lanes = pl.ds(pl.multiple_of(b * 128, 128), 128)
        rmask[:, lanes] = hot(iota((NODES, 128), 0) == mrow_ref[:, lanes])
        return carry

    lax.fori_loop(0, MEDGES // 128, masks, 0)

    centre("wpo")
    w_copies["wpe"].wait()
    wcat[...] = jnp.zeros_like(wcat)
    wcat[0:4, 0:L] = wmf_ref[...].astype(F32)
    wcat[:, L : 2 * L] = dot(wcat[:, 0:L].astype(BF16), weight("wpe"))

    def landed(k):
        return pltpu.make_async_remote_copy(
            src_ref=eout.at[k],
            dst_ref=ein.at[k],
            send_sem=es_sem.at[k],
            recv_sem=er_sem.at[k],
            device_id=near_id(CODES[0]),
            device_id_type=MESH,
        )

    def arrive(g, carry):
        for i in range(2):
            landed(2 * g + i).wait_recv()
        mbuf[...] += encode(ein[pl.ds(2 * g, 2)], 2)
        return carry

    lax.fori_loop(0, 4, arrive, 0)

    w_copies["wni"].wait()
    w_copies["wno"].wait()
    h = silu(dot(mbuf[...].astype(BF16), weight("wni"))).astype(BF16)
    latent = normalize(dot(h, weight("wno"))).astype(BF16)
    lat_buf[...] = latent
    w_copies["wps"].wait()
    own = dot(latent, weight("wps")).astype(BF16)
    tpre[0:NODES, :] = own

    def a1_copy(i):
        other, device = a_peer(i)
        return pltpu.make_async_remote_copy(
            src_ref=a1_out.at[other], dst_ref=a1_in.at[zx],
            send_sem=a1s.at[i], recv_sem=a1r.at[i], device_id=device, device_id_type=MESH,
        )

    def b1_copy(i):
        other, device = b_peer(i)
        return pltpu.make_async_remote_copy(
            src_ref=b1_out.at[other], dst_ref=b1_in.at[spot],
            send_sem=b1s.at[i], recv_sem=b1r.at[i], device_id=device, device_id_type=MESH,
        )

    def a2_copy(i):
        other, device = a_peer(i)
        return pltpu.make_async_remote_copy(
            src_ref=a2_out.at[other], dst_ref=a2_in.at[zx],
            send_sem=a2s.at[i], recv_sem=a2r.at[i], device_id=device, device_id_type=MESH,
        )

    def b2_copy(i):
        other, device = b_peer(i)
        return pltpu.make_async_remote_copy(
            src_ref=b2_out.at[other], dst_ref=b2_in.at[spot],
            send_sem=b2s.at[i], recv_sem=b2r.at[i], device_id=device, device_id_type=MESH,
        )

    def each(count, make, act):
        def step(i, carry):
            act(make(i))
            return carry

        lax.fori_loop(1, count, step, 0)

    def start(copy):
        copy.start()

    def arrived(copy):
        copy.wait_recv()

    def gone(copy):
        copy.wait_send()

    b1_out[...] = dot(gsend[768:1024, :], own[:, 256:512]).astype(BF16).reshape(8, 32, 256)
    each(8, b1_copy, start)
    a1_out[...] = dot(gsend[512:768, :], own[:, 0:256]).astype(BF16).reshape(16, 16, 256)
    each(16, a1_copy, start)

    def near_copy(e):
        return pltpu.make_async_remote_copy(
            src_ref=near_out.at[e],
            dst_ref=tnear.at[7 - e],
            send_sem=ns_sem.at[e],
            recv_sem=nr_sem.at[e],
            device_id=near_id(e if e < 4 else e + 1),
            device_id_type=MESH,
        )

    near_out[...] = dot(gsend[0:512, :], own).astype(BF16).reshape(8, HCAP, L)
    for e in (0, 2, 5, 7, 3, 4, 1, 6):
        near_copy(e).start()
    a1_in[zx] = a1_out[zx]
    b1_in[spot] = b1_out[spot]

    w_copies["wpr"].wait()
    tpre[NODES : 2 * NODES, :] = dot(latent, weight("wpr")).astype(BF16)

    def ahead(b, carry):
        rows = pl.ds(pl.multiple_of(b * BLK, BLK), BLK)
        embed = dot_tn(featp[:, rows].astype(BF16), wcat[...].astype(BF16))
        obuf[rows, :] = embed[:, 0:L].astype(BF16)
        pre[rows, :] = dot(apre[rows, :], tpre[...]) + embed[:, L : 2 * L]
        return carry

    lax.fori_loop(0, AHEAD, ahead, 0)

    each(8, b1_copy, arrived)
    to_zx = hot(iota((256, 256), 1) == far_order(0))
    a2_out[...] = dot(to_zx, b1_in[...].reshape(256, 256)).astype(BF16).reshape(16, 16, 256)
    each(16, a2_copy, start)
    each(16, a1_copy, arrived)
    to_spot = hot(iota((256, 256), 1) == far_order(1))
    b2_out[...] = dot(to_spot, a1_in[...].reshape(256, 256)).astype(BF16).reshape(8, 32, 256)
    each(8, b2_copy, start)
    a2_in[zx] = a2_out[zx]
    b2_in[spot] = b2_out[spot]

    lax.fori_loop(AHEAD, NBLK, ahead, 0)

    for e in range(8):
        near_copy(e).wait_recv()

    def near_part(b, carry):
        rows = pl.ds(pl.multiple_of(b * BLK, BLK), BLK)
        pre[rows, :] += dot(apost[rows, 0:512], tnear[...].reshape(512, L))
        return carry

    lax.fori_loop(0, NBLK, near_part, 0)

    each(16, a2_copy, arrived)
    each(8, b2_copy, arrived)
    tfar[:, 0:256] = dot(to_zx, b2_in[...].reshape(256, 256)).astype(BF16)
    tfar[:, 256:512] = a2_in[...].reshape(256, 256)

    mbuf[...] = jnp.zeros_like(mbuf)

    def out_copy(b):
        rows = pl.ds(pl.multiple_of(b * BLK, BLK), BLK)
        return pltpu.make_async_copy(obuf.at[rows], edge_out.at[rows], o_sem.at[b])

    def hidden(b):
        rows = pl.ds(pl.multiple_of(b * BLK, BLK), BLK)
        return silu(pre[rows, :] + dot(apost[rows, 512:768], tfar[...])).astype(BF16)

    def finish(b, h):
        rows = pl.ds(pl.multiple_of(b * BLK, BLK), BLK)
        return (obuf[rows, :].astype(F32) + scaled(dot(h, weight("wpo")))).astype(BF16)

    hbuf[0] = hidden(0)

    def process(b, carry):
        rows = pl.ds(pl.multiple_of(b * BLK, BLK), BLK)
        out = finish(b, hbuf[lax.rem(b, 2)])
        ahead_h = hidden(b + 1)
        total = mbuf[...] + dot(rmask[:, rows], out)
        obuf[rows, :] = out
        hbuf[lax.rem(b + 1, 2)] = ahead_h
        mbuf[...] = total
        out_copy(b).start()
        return carry

    lax.fori_loop(0, NBLK - 1, process, 0)
    last = NBLK - 1
    out = finish(last, hbuf[last % 2])
    obuf[last * BLK : MEDGES, :] = out
    out_copy(last).start()
    edge_sum = (mbuf[...] + dot(rmask[:, last * BLK : MEDGES], out)).astype(BF16)

    w_copies["wus"].wait()
    w_copies["wua"].wait()
    w_copies["wuo"].wait()
    h = dot(lat_buf[...], weight("wus")) + dot(edge_sum, weight("wua"))
    h = silu(h).astype(BF16)
    mesh_out[...] = (lat_buf[...].astype(F32) + normalize(dot(h, weight("wuo")))).astype(BF16)

    for k in range(8):
        edge_copy(k).wait_send()
        near_copy(k).wait_send()

    each(16, a1_copy, gone)
    each(8, b1_copy, gone)
    each(16, a2_copy, gone)
    each(8, b2_copy, gone)

    def o_sent(b, carry):
        out_copy(b).wait()
        return carry

    lax.fori_loop(0, NBLK, o_sent, 0)


def on_device(
    grid_in, g2m_senders, g2m_dest, g2m_receivers, g2m_feat, halo_near, halo_far, mesh_senders,
    mesh_receivers, mesh_feat, w_grid_in, w_grid_out, w_edge_latent, w_edge_feat, w_edge_out, w_node_in,
    w_node_out, w_mesh_feat, w_proc_edge, w_proc_send, w_proc_recv, w_proc_out, w_upd_self, w_upd_sum,
    w_upd_out,
):
    vm = pl.BlockSpec(memory_space=pltpu.VMEM)
    hb = pl.BlockSpec(memory_space=pl.ANY)
    dma = pltpu.SemaphoreType.DMA
    return pl.pallas_call(
        kernel,
        out_shape=(
            jax.ShapeDtypeStruct((NODES, L), BF16),
            jax.ShapeDtypeStruct((MEDGES, L), BF16),
        ),
        in_specs=[hb, vm, vm, vm, vm, vm, vm, vm, vm, vm, hb, vm, vm] + [hb] * 12,
        out_specs=(vm, hb),
        scratch_shapes=[
            pltpu.VMEM((128, 128), I32),
            pltpu.VMEM((1, MEDGES), I32),
            pltpu.VMEM((CIN, GRID_N), BF16),
            pltpu.VMEM((EDGES, 256), BF16),
            pltpu.VMEM((CIN, L), BF16),
            pltpu.VMEM((256, L), F32),
            pltpu.VMEM((256, L), BF16),
            pltpu.VMEM((12, L, L), BF16),
            pltpu.VMEM((16, EDGES), F32),
            pltpu.VMEM((16, L), F32),
            pltpu.VMEM((16, MEDGES), F32),
            pltpu.VMEM((16, 2 * L), F32),
            pltpu.VMEM((8, SLOT, 256), BF16),
            pltpu.VMEM((9, SLOT, 256), BF16),
            pltpu.VMEM((MEDGES // 128, 128, 128), I32),
            pltpu.VMEM((MEDGES // 128, 128, 128), I32),
            pltpu.VMEM((MEDGES, 2 * NODES), BF16),
            pltpu.VMEM((MEDGES, 768), BF16),
            pltpu.VMEM((NODES, MEDGES), BF16),
            pltpu.VMEM((1024, NODES), BF16),
            pltpu.VMEM((2 * NODES, L), BF16),
            pltpu.VMEM((8, HCAP, L), BF16),
            pltpu.VMEM((256, L), BF16),
            pltpu.VMEM((8, HCAP, L), BF16),
            pltpu.VMEM((16, 16, 256), BF16),
            pltpu.VMEM((16, 16, 256), BF16),
            pltpu.VMEM((8, 32, 256), BF16),
            pltpu.VMEM((8, 32, 256), BF16),
            pltpu.VMEM((8, 32, 256), BF16),
            pltpu.VMEM((8, 32, 256), BF16),
            pltpu.VMEM((16, 16, 256), BF16),
            pltpu.VMEM((16, 16, 256), BF16),
            pltpu.VMEM((2, BLK, L), BF16),
            pltpu.VMEM((MEDGES, L), F32),
            pltpu.VMEM((MEDGES, L), BF16),
            pltpu.VMEM((NODES, L), BF16),
            pltpu.VMEM((NODES, L), F32),
            dma((2,)),
            dma((12,)),
            dma((8,)),
            dma((8,)),
            dma((8,)),
            dma((8,)),
            dma((16,)),
            dma((16,)),
            dma((8,)),
            dma((8,)),
            dma((8,)),
            dma((8,)),
            dma((16,)),
            dma((16,)),
            dma((NBLK,)),
        ],
        compiler_params=pltpu.CompilerParams(
            collective_id=0, has_side_effects=True, vmem_limit_bytes=60 * 1024 * 1024
        ),
        cost_estimate=pl.CostEstimate(flops=15_000_000_000, bytes_accessed=12_000_000, transcendentals=4_000_000),
    )(
        grid_in.T, g2m_senders, g2m_dest.reshape(1, EDGES), g2m_receivers, g2m_feat,
        halo_near.reshape(8, HCAP), halo_far.reshape(128, 2).T, mesh_senders, mesh_receivers, mesh_feat, w_grid_in, w_edge_feat, w_mesh_feat,
        w_grid_out, w_edge_latent, w_edge_out, w_node_in, w_node_out, w_proc_edge, w_proc_send, w_proc_recv,
        w_proc_out, w_upd_self, w_upd_sum, w_upd_out,
    )


def solution(mesh):
    both = ("lat", "lon")
    rows, flat, cube = P(both, None), P(both), P(both, None, None)
    return jax.shard_map(
        on_device,
        mesh=mesh,
        in_specs=(rows, flat, rows, flat, P(None, both), cube, cube, flat, flat, P(None, both)) + (P(),) * 15,
        out_specs=(rows, rows),
        check_vma=False,
    )
```

```python
import functools

import jax
import jax.numpy as jnp
from jax import lax
from jax.experimental import pallas as pl
from jax.experimental.pallas import tpu as pltpu
from jax.sharding import PartitionSpec as P

F32 = jnp.float32
BF16 = jnp.bfloat16
I32 = jnp.int32
MESH = pl.DeviceIdType.MESH

N_LAT, N_LON = 32, 4
L = 512
CIN = 227
GRID_N = 1024
EDGES = 768
NODES = 320
MEDGES = 2560
CAP = 192
HCAP = 64
SLOT = CAP + 16
TALL = 1280
BLK = 640
NBLK = MEDGES // BLK

CODES = (1, 7, 3, 5, 0, 2, 6, 8)
SEND_ORDER = (2, 3, 0, 1, 4, 5, 6, 7)

COL_SEND = 0
COL_NEAR = 6
COL_FAR = 10
COL_MS = 12
COL_MR = 32

W_NAMES = (
    "wgo", "wel", "weo", "wni", "wno", "wpe", "wps", "wpr", "wpo", "wus", "wua", "wuo",
)


def dot(a, b):
    return jnp.dot(a, b, preferred_element_type=F32)


def dot_tn(a, b):
    return lax.dot_general(a, b, (((0,), (0,)), ((), ())), preferred_element_type=F32)


def dot_nt(a, b):
    return lax.dot_general(a, b, (((1,), (1,)), ((), ())), preferred_element_type=F32)


def silu(v):
    h = 0.5 * v
    return h + h * jnp.tanh(h)


def scaled(v):
    return v * lax.rsqrt(jnp.mean(v * v, axis=-1, keepdims=True) + 1e-05)


def normalize(v):
    c = v - jnp.mean(v, axis=-1, keepdims=True)
    return c * lax.rsqrt(jnp.mean(c * c, axis=-1, keepdims=True) + 1e-05)


def far_order(kind):
    j = iota((256, 256), 0)
    row = lax.bitwise_and(j, 1)
    if kind == 0:
        return lax.bitwise_and(lax.shift_right_logical(j, 1), 7) * 32 + lax.shift_right_logical(j, 4) * 2 + row
    return lax.bitwise_and(lax.shift_right_logical(j, 1), 15) * 16 + lax.shift_right_logical(j, 5) * 2 + row


def iota(shape, dim):
    return lax.broadcasted_iota(I32, shape, dim)


def hot(mask):
    return jnp.where(mask, 1.0, 0.0).astype(BF16)


def kernel(
    grid_hbm, send_ref, dest_ref, recv_ref, gfeat_ref, near_ref, far_ref, msend_ref, mrecv_ref, mfeat_ref,
    wgi_hbm, wef_ref, wmf_ref,
    wgo_h, wel_h, weo_h, wni_h, wno_h, wpe_h, wps_h, wpr_h, wpo_h, wus_h, wua_h, wuo_h,
    mesh_out, edge_out,
    idx, mrow_ref, graw, pick, gsel, wraw, wpad32, wgi, wts, aux, wefp, featp, wmf,
    eout, ein, scol, rcol, apre, apost, rmask, gsend,
    tpre, tnear, tfar, near_out, a1_out, a1_in, b1_out, b1_in, b2_out, b2_in, a2_out, a2_in, hbuf,
    pre, obuf, lat_buf, mbuf,
    in_sem, w_sem, es_sem, er_sem, ns_sem, nr_sem, a1s, a1r, b1s, b1r, b2s, b2r, a2s, a2r, o_sem,
):
    lat = lax.axis_index("lat")
    lon = lax.axis_index("lon")
    zx = lax.div(lat, 2)
    core = lax.rem(lat, 2)
    spot = core * 4 + lon

    def near_id(code):
        return (
            lax.rem(lat + (code // 3 - 1) + N_LAT, N_LAT),
            lax.rem(lon + (code % 3 - 1) + N_LON, N_LON),
        )

    def a_peer(i):
        other = lax.rem(zx + i, 16)
        return other, (other * 2 + core, lon)

    def b_peer(i):
        other = lax.rem(spot + i, 8)
        return other, (zx * 2 + lax.div(other, 4), lax.rem(other, 4))

    barrier = pltpu.get_barrier_semaphore()
    for code in CODES:
        pl.semaphore_signal(barrier, inc=1, device_id=near_id(code), device_id_type=MESH)

    def greet_a(i, carry):
        pl.semaphore_signal(barrier, inc=1, device_id=a_peer(i)[1], device_id_type=MESH)
        return carry

    def greet_b(i, carry):
        pl.semaphore_signal(barrier, inc=1, device_id=b_peer(i)[1], device_id_type=MESH)
        return carry

    lax.fori_loop(1, 16, greet_a, 0)
    lax.fori_loop(1, 8, greet_b, 0)

    g_copy = pltpu.make_async_copy(grid_hbm, graw, in_sem.at[0])
    g_copy.start()
    wi_copy = pltpu.make_async_copy(wgi_hbm, wraw, in_sem.at[1])
    wi_copy.start()
    w_copies = {}
    for k, (name, ref) in enumerate(
        zip(W_NAMES, (wgo_h, wel_h, weo_h, wni_h, wno_h, wpe_h, wps_h, wpr_h, wpo_h, wus_h, wua_h, wuo_h))
    ):
        w_copies[name] = pltpu.make_async_copy(ref, wts.at[k], w_sem.at[k])
        w_copies[name].start()

    def weight(name):
        return wts[W_NAMES.index(name)]

    codes = dest_ref[...]
    marks = jnp.where(iota((16, EDGES), 0) == codes, 1.0, 0.0)
    below = hot(iota((EDGES, EDGES), 0) < iota((EDGES, EDGES), 1))
    earlier = dot(marks.astype(BF16), below)
    rank = jnp.sum(earlier * marks, axis=0, keepdims=True).astype(I32)
    place = codes * CAP + rank

    name_row = recv_ref[...].reshape(1, EDGES) + 1
    aux[...] = jnp.zeros_like(aux)
    aux[0:1, :] = lax.shift_right_logical(name_row, 4).astype(F32)
    aux[1:2, :] = lax.bitwise_and(name_row, 15).astype(F32)
    aux[4:8, :] = gfeat_ref[...].astype(F32)
    aux_rows = aux[...].astype(BF16)

    idx[COL_SEND : COL_SEND + 6, :] = send_ref[...].reshape(6, 128)
    for e in range(8):
        idx[COL_NEAR + e // 2 : COL_NEAR + e // 2 + 1, e % 2 * 64 : e % 2 * 64 + 64] = near_ref[e : e + 1, :]
    idx[COL_FAR : COL_FAR + 2, :] = far_ref[...]
    idx[COL_MS : COL_MS + 20, :] = msend_ref[...].reshape(20, 128)
    idx[COL_MR : COL_MR + 20, :] = mrecv_ref[...].reshape(20, 128)
    idx[COL_MR + 20 :, :] = jnp.zeros((128 - COL_MR - 20, 128), I32)
    mrow_ref[...] = mrecv_ref[...].reshape(1, MEDGES)
    idx_t = jnp.transpose(idx[...])

    g_copy.wait()
    gsel[:, 128:256] = jnp.zeros((EDGES, 128), BF16)
    for b in range(EDGES // 128):
        pick[b * 128 : (b + 1) * 128, :] = hot(idx_t[:, COL_SEND + b : COL_SEND + b + 1] == iota((128, GRID_N), 1))
    gsel[:, 0:CIN] = dot_nt(pick[...], graw[...]).astype(BF16)

    def choice(code):
        return hot(iota((CAP, EDGES), 0) + code * CAP == place)

    def pack(jobs):
        choose = jnp.concatenate([choice(code) for code, _, _ in jobs], axis=0)
        rows = dot(choose, gsel[...]).astype(BF16)
        tails = dot_nt(aux_rows, choose).astype(BF16)
        for i, (_, target, k) in enumerate(jobs):
            target[k, 0:CAP, :] = rows[i * CAP : (i + 1) * CAP]
            target[k, CAP:SLOT, :] = jnp.zeros((16, 256), BF16)
            target[k, CAP:SLOT, 0:CAP] = tails[:, i * CAP : (i + 1) * CAP]

    def edge_copy(k):
        return pltpu.make_async_remote_copy(
            src_ref=eout.at[k],
            dst_ref=ein.at[k],
            send_sem=es_sem.at[k],
            recv_sem=er_sem.at[k],
            device_id=near_id(CODES[k]),
            device_id_type=MESH,
        )

    for n in range(0, 8, 4):
        pack([(CODES[k], eout, k) for k in SEND_ORDER[n : n + 4]])
        if n == 0:
            pl.semaphore_wait(barrier, 8 + 15 + 7)
        for k in SEND_ORDER[n : n + 4]:
            edge_copy(k).start()
    pack([(4, ein, 8)])

    wi_copy.wait()
    wpad32[224:256, :] = jnp.zeros((32, L), F32)
    wpad32[0:CIN, :] = wraw[...].astype(F32)
    wgi[...] = wpad32[...].astype(BF16)
    wefp[...] = jnp.zeros_like(wefp)
    wefp[4:8, :] = wef_ref[...].astype(F32)

    def centre(name):
        w_copies[name].wait()
        w = weight(name).astype(F32)
        wts[W_NAMES.index(name)] = (w - jnp.mean(w, axis=-1, keepdims=True)).astype(BF16)

    centre("wgo")
    w_copies["wel"].wait()
    centre("weo")

    def encode(slots, count):
        wf = wefp[...].astype(BF16)
        tails = [slots[i, CAP:SLOT, :][:, 0:CAP] for i in range(count)]
        v = dot(slots[:, 0:CAP, :].reshape(count * CAP, 256), wgi[...])
        v = dot(silu(v).astype(BF16), weight("wgo"))
        v = dot(scaled(v).astype(BF16), weight("wel"))
        feat = [dot_tn(t, wf) for t in tails]
        v = v + (jnp.concatenate(feat, axis=0) if count > 1 else feat[0])
        message = scaled(dot(silu(v).astype(BF16), weight("weo"))).astype(BF16)
        total = None
        for i, t in enumerate(tails):
            t = t.astype(F32)
            node = (t[0:1, :] * 16.0 + t[1:2, :] - 1.0).astype(I32)
            part = dot(hot(iota((NODES, CAP), 0) == node), message[i * CAP : (i + 1) * CAP])
            total = part if total is None else total + part
        return total

    mbuf[...] = encode(ein[8:9], 1)

    for b in range(MEDGES // 128):
        scol[b] = jnp.broadcast_to(idx_t[:, COL_MS + b : COL_MS + b + 1], (128, 128))
        rcol[b] = jnp.broadcast_to(idx_t[:, COL_MR + b : COL_MR + b + 1], (128, 128))
    def node_hot(c):
        return hot(idx_t[:, c : c + 1] == iota((128, NODES), 1))

    for b in range(4):
        gsend[b * 128 : (b + 1) * 128, :] = node_hot(COL_NEAR + b)
    j = iota((256, 256), 0)
    k = iota((256, 256), 1)
    j_row = lax.bitwise_and(j, 1)
    j_zx = lax.bitwise_and(lax.shift_right_logical(j, 1), 15)
    j_spot = lax.shift_right_logical(j, 5)
    far_hot = jnp.concatenate([node_hot(COL_FAR), node_hot(COL_FAR + 1)], axis=0)
    gsend[512:768, :] = dot(hot(k == j_row * 128 + lax.shift_right_logical(j, 1)), far_hot).astype(BF16)
    gsend[768:1024, :] = dot(hot(k == j_row * 128 + j_zx * 8 + j_spot), far_hot).astype(BF16)

    featp[...] = jnp.zeros_like(featp)
    featp[0:4, :] = mfeat_ref[...].astype(F32)
    apre[:, 640:768] = jnp.zeros((MEDGES, 128), BF16)

    def masks(b, carry):
        s = scol[b]
        r = rcol[b]
        lane = iota((128, 128), 1)
        rows = pl.ds(pl.multiple_of(b * 128, 128), 128)
        for t in range(5):
            if t < 2:
                m = s == lane + t * 128
            elif t == 2:
                m = ((s == lane + 256) & (lane < 64)) | (r == lane - 64)
            else:
                m = r == lane + (t * 128 - NODES)
            apre[rows, t * 128 : (t + 1) * 128] = hot(m)
        for t in range(4):
            apost[rows, t * 128 : (t + 1) * 128] = hot(s == lane + (NODES + t * 128))
        f = s - (NODES + 8 * HCAP)
        for t in range(2):
            apost[rows, 512 + t * 128 : 512 + (t + 1) * 128] = hot(f == lane + t * 128)
        lanes = pl.ds(pl.multiple_of(b * 128, 128), 128)
        apre[rows, 640:648] = jnp.transpose(featp[:, lanes]).astype(BF16)
        rmask[:, lanes] = hot(iota((NODES, 128), 0) == mrow_ref[:, lanes])
        return carry

    lax.fori_loop(0, MEDGES // 128, masks, 0)

    centre("wpo")
    w_copies["wpe"].wait()
    wmf[...] = jnp.zeros_like(wmf)
    wmfp = jnp.concatenate([wmf_ref[...].astype(F32), jnp.zeros((12, L), F32)], axis=0).astype(BF16)
    wmf[0:16, :] = wmfp
    tpre[640:768, :] = jnp.zeros((128, L), BF16)
    tpre[640:656, :] = dot(wmfp, weight("wpe")).astype(BF16)

    def landed(k):
        return pltpu.make_async_remote_copy(
            src_ref=eout.at[k],
            dst_ref=ein.at[k],
            send_sem=es_sem.at[k],
            recv_sem=er_sem.at[k],
            device_id=near_id(CODES[0]),
            device_id_type=MESH,
        )

    def arrive(g, carry):
        for i in range(4):
            landed(4 * g + i).wait_recv()
        mbuf[...] += encode(ein[pl.ds(4 * g, 4)], 4)
        return carry

    lax.fori_loop(0, 2, arrive, 0)

    w_copies["wni"].wait()
    w_copies["wno"].wait()
    h = silu(dot(mbuf[...].astype(BF16), weight("wni"))).astype(BF16)
    latent = normalize(dot(h, weight("wno"))).astype(BF16)
    lat_buf[...] = latent
    w_copies["wps"].wait()
    own = dot(latent, weight("wps")).astype(BF16)
    tpre[0:NODES, :] = own

    def a1_copy(i):
        other, device = a_peer(i)
        return pltpu.make_async_remote_copy(
            src_ref=a1_out.at[other], dst_ref=a1_in.at[zx],
            send_sem=a1s.at[i], recv_sem=a1r.at[i], device_id=device, device_id_type=MESH,
        )

    def b1_copy(i):
        other, device = b_peer(i)
        return pltpu.make_async_remote_copy(
            src_ref=b1_out.at[other], dst_ref=b1_in.at[spot],
            send_sem=b1s.at[i], recv_sem=b1r.at[i], device_id=device, device_id_type=MESH,
        )

    def a2_copy(i):
        other, device = a_peer(i)
        return pltpu.make_async_remote_copy(
            src_ref=a2_out.at[other], dst_ref=a2_in.at[zx],
            send_sem=a2s.at[i], recv_sem=a2r.at[i], device_id=device, device_id_type=MESH,
        )

    def b2_copy(i):
        other, device = b_peer(i)
        return pltpu.make_async_remote_copy(
            src_ref=b2_out.at[other], dst_ref=b2_in.at[spot],
            send_sem=b2s.at[i], recv_sem=b2r.at[i], device_id=device, device_id_type=MESH,
        )

    def each(count, make, act):
        def step(i, carry):
            act(make(i))
            return carry

        lax.fori_loop(1, count, step, 0)

    def start(copy):
        copy.start()

    def arrived(copy):
        copy.wait_recv()

    def gone(copy):
        copy.wait_send()

    b1_out[...] = dot(gsend[768:1024, :], own[:, 256:512]).astype(BF16).reshape(8, 32, 256)
    each(8, b1_copy, start)
    a1_out[...] = dot(gsend[512:768, :], own[:, 0:256]).astype(BF16).reshape(16, 16, 256)
    each(16, a1_copy, start)

    def near_copy(e):
        return pltpu.make_async_remote_copy(
            src_ref=near_out.at[e],
            dst_ref=tnear.at[7 - e],
            send_sem=ns_sem.at[e],
            recv_sem=nr_sem.at[e],
            device_id=near_id(e if e < 4 else e + 1),
            device_id_type=MESH,
        )

    near_out[...] = dot(gsend[0:512, :], own).astype(BF16).reshape(8, HCAP, L)
    for e in (0, 2, 5, 7, 3, 4, 1, 6):
        near_copy(e).start()
    a1_in[zx] = a1_out[zx]
    b1_in[spot] = b1_out[spot]

    w_copies["wpr"].wait()
    tpre[NODES : 2 * NODES, :] = dot(latent, weight("wpr")).astype(BF16)

    def tall(b):
        return pl.ds(pl.multiple_of(b * TALL, TALL), TALL)

    def ahead(b, carry):
        obuf[tall(b), :] = dot(apre[tall(b), 640:768], wmf[...]).astype(BF16)
        pre[tall(b), :] = dot(apre[tall(b), :], tpre[...])
        return carry

    ahead(0, 0)

    each(8, b1_copy, arrived)
    to_zx = hot(iota((256, 256), 1) == far_order(0))
    a2_out[...] = dot(to_zx, b1_in[...].reshape(256, 256)).astype(BF16).reshape(16, 16, 256)
    each(16, a2_copy, start)
    each(16, a1_copy, arrived)
    to_spot = hot(iota((256, 256), 1) == far_order(1))
    b2_out[...] = dot(to_spot, a1_in[...].reshape(256, 256)).astype(BF16).reshape(8, 32, 256)
    each(8, b2_copy, start)
    a2_in[zx] = a2_out[zx]
    b2_in[spot] = b2_out[spot]

    ahead(1, 0)

    for e in range(8):
        near_copy(e).wait_recv()

    def near_part(b, carry):
        pre[tall(b), :] += dot(apost[tall(b), 0:512], tnear[...].reshape(512, L))
        return carry

    lax.fori_loop(0, MEDGES // TALL, near_part, 0)

    each(16, a2_copy, arrived)
    each(8, b2_copy, arrived)
    tfar[:, 0:256] = dot(to_zx, b2_in[...].reshape(256, 256)).astype(BF16)
    tfar[:, 256:512] = a2_in[...].reshape(256, 256)

    mbuf[...] = jnp.zeros_like(mbuf)

    def out_copy(b):
        rows = pl.ds(pl.multiple_of(b * BLK, BLK), BLK)
        return pltpu.make_async_copy(obuf.at[rows], edge_out.at[rows], o_sem.at[b])

    def hidden(b):
        rows = pl.ds(pl.multiple_of(b * BLK, BLK), BLK)
        return silu(pre[rows, :] + dot(apost[rows, 512:768], tfar[...])).astype(BF16)

    def finish(b, h):
        rows = pl.ds(pl.multiple_of(b * BLK, BLK), BLK)
        return (obuf[rows, :].astype(F32) + scaled(dot(h, weight("wpo")))).astype(BF16)

    hbuf[0] = hidden(0)

    def process(b, carry):
        rows = pl.ds(pl.multiple_of(b * BLK, BLK), BLK)
        out = finish(b, hbuf[lax.rem(b, 2)])
        ahead_h = hidden(b + 1)
        total = mbuf[...] + dot(rmask[:, rows], out)
        obuf[rows, :] = out
        hbuf[lax.rem(b + 1, 2)] = ahead_h
        mbuf[...] = total
        out_copy(b).start()
        return carry

    lax.fori_loop(0, NBLK - 1, process, 0)
    last = NBLK - 1
    out = finish(last, hbuf[last % 2])
    obuf[last * BLK : MEDGES, :] = out
    out_copy(last).start()
    edge_sum = (mbuf[...] + dot(rmask[:, last * BLK : MEDGES], out)).astype(BF16)

    w_copies["wus"].wait()
    w_copies["wua"].wait()
    w_copies["wuo"].wait()
    h = dot(lat_buf[...], weight("wus")) + dot(edge_sum, weight("wua"))
    h = silu(h).astype(BF16)
    mesh_out[...] = (lat_buf[...].astype(F32) + normalize(dot(h, weight("wuo")))).astype(BF16)

    for k in range(8):
        edge_copy(k).wait_send()
        near_copy(k).wait_send()

    each(16, a1_copy, gone)
    each(8, b1_copy, gone)
    each(16, a2_copy, gone)
    each(8, b2_copy, gone)

    def o_sent(b, carry):
        out_copy(b).wait()
        return carry

    lax.fori_loop(0, NBLK, o_sent, 0)


def on_device(
    grid_in, g2m_senders, g2m_dest, g2m_receivers, g2m_feat, halo_near, halo_far, mesh_senders,
    mesh_receivers, mesh_feat, w_grid_in, w_grid_out, w_edge_latent, w_edge_feat, w_edge_out, w_node_in,
    w_node_out, w_mesh_feat, w_proc_edge, w_proc_send, w_proc_recv, w_proc_out, w_upd_self, w_upd_sum,
    w_upd_out,
):
    vm = pl.BlockSpec(memory_space=pltpu.VMEM)
    hb = pl.BlockSpec(memory_space=pl.ANY)
    dma = pltpu.SemaphoreType.DMA
    return pl.pallas_call(
        kernel,
        out_shape=(
            jax.ShapeDtypeStruct((NODES, L), BF16),
            jax.ShapeDtypeStruct((MEDGES, L), BF16),
        ),
        in_specs=[hb, vm, vm, vm, vm, vm, vm, vm, vm, vm, hb, vm, vm] + [hb] * 12,
        out_specs=(vm, hb),
        scratch_shapes=[
            pltpu.VMEM((128, 128), I32),
            pltpu.VMEM((1, MEDGES), I32),
            pltpu.VMEM((CIN, GRID_N), BF16),
            pltpu.VMEM((EDGES, GRID_N), BF16),
            pltpu.VMEM((EDGES, 256), BF16),
            pltpu.VMEM((CIN, L), BF16),
            pltpu.VMEM((256, L), F32),
            pltpu.VMEM((256, L), BF16),
            pltpu.VMEM((12, L, L), BF16),
            pltpu.VMEM((16, EDGES), F32),
            pltpu.VMEM((16, L), F32),
            pltpu.VMEM((8, MEDGES), F32),
            pltpu.VMEM((128, L), BF16),
            pltpu.VMEM((8, SLOT, 256), BF16),
            pltpu.VMEM((9, SLOT, 256), BF16),
            pltpu.VMEM((MEDGES // 128, 128, 128), I32),
            pltpu.VMEM((MEDGES // 128, 128, 128), I32),
            pltpu.VMEM((MEDGES, 768), BF16),
            pltpu.VMEM((MEDGES, 768), BF16),
            pltpu.VMEM((NODES, MEDGES), BF16),
            pltpu.VMEM((1024, NODES), BF16),
            pltpu.VMEM((768, L), BF16),
            pltpu.VMEM((8, HCAP, L), BF16),
            pltpu.VMEM((256, L), BF16),
            pltpu.VMEM((8, HCAP, L), BF16),
            pltpu.VMEM((16, 16, 256), BF16),
            pltpu.VMEM((16, 16, 256), BF16),
            pltpu.VMEM((8, 32, 256), BF16),
            pltpu.VMEM((8, 32, 256), BF16),
            pltpu.VMEM((8, 32, 256), BF16),
            pltpu.VMEM((8, 32, 256), BF16),
            pltpu.VMEM((16, 16, 256), BF16),
            pltpu.VMEM((16, 16, 256), BF16),
            pltpu.VMEM((2, BLK, L), BF16),
            pltpu.VMEM((MEDGES, L), F32),
            pltpu.VMEM((MEDGES, L), BF16),
            pltpu.VMEM((NODES, L), BF16),
            pltpu.VMEM((NODES, L), F32),
            dma((2,)),
            dma((12,)),
            dma((8,)),
            dma((8,)),
            dma((8,)),
            dma((8,)),
            dma((16,)),
            dma((16,)),
            dma((8,)),
            dma((8,)),
            dma((8,)),
            dma((8,)),
            dma((16,)),
            dma((16,)),
            dma((NBLK,)),
        ],
        compiler_params=pltpu.CompilerParams(
            collective_id=0, has_side_effects=True, vmem_limit_bytes=60 * 1024 * 1024
        ),
        cost_estimate=pl.CostEstimate(flops=15_000_000_000, bytes_accessed=12_000_000, transcendentals=4_000_000),
    )(
        grid_in.T, g2m_senders, g2m_dest.reshape(1, EDGES), g2m_receivers, g2m_feat,
        halo_near.reshape(8, HCAP), halo_far.reshape(128, 2).T, mesh_senders, mesh_receivers, mesh_feat, w_grid_in, w_edge_feat, w_mesh_feat,
        w_grid_out, w_edge_latent, w_edge_out, w_node_in, w_node_out, w_proc_edge, w_proc_send, w_proc_recv,
        w_proc_out, w_upd_self, w_upd_sum, w_upd_out,
    )


def solution(mesh):
    both = ("lat", "lon")
    rows, flat, cube = P(both, None), P(both), P(both, None, None)
    return jax.shard_map(
        on_device,
        mesh=mesh,
        in_specs=(rows, flat, rows, flat, P(None, both), cube, cube, flat, flat, P(None, both)) + (P(),) * 15,
        out_specs=(rows, rows),
        check_vma=False,
    )
```

```python
import functools

import jax
import jax.numpy as jnp
from jax import lax
from jax.experimental import pallas as pl
from jax.experimental.pallas import tpu as pltpu
from jax.sharding import PartitionSpec as P

F32 = jnp.float32
BF16 = jnp.bfloat16
I32 = jnp.int32
MESH = pl.DeviceIdType.MESH

N_LAT, N_LON = 32, 4
L = 512
CIN = 227
GRID_N = 1024
EDGES = 768
NODES = 320
MEDGES = 2560
CAP = 192
HCAP = 64
SLOT = CAP + 16
TALL = 1280
PIECES = 8
BLK = 640
NBLK = MEDGES // BLK

CODES = (1, 7, 3, 5, 0, 2, 6, 8)
SEND_ORDER = (2, 3, 0, 1, 4, 5, 6, 7)

COL_SEND = 0
COL_NEAR = 6
COL_FAR = 10
COL_MS = 12
COL_MR = 32

W_NAMES = (
    "wgo", "wel", "weo", "wni", "wno", "wpe", "wps", "wpr", "wpo", "wus", "wua", "wuo",
)


def dot(a, b):
    return jnp.dot(a, b, preferred_element_type=F32)


def dot_tn(a, b):
    return lax.dot_general(a, b, (((0,), (0,)), ((), ())), preferred_element_type=F32)


def dot_nt(a, b):
    return lax.dot_general(a, b, (((1,), (1,)), ((), ())), preferred_element_type=F32)


def silu(v):
    h = 0.5 * v
    return h + h * jnp.tanh(h)


def scaled(v):
    return v * lax.rsqrt(jnp.mean(v * v, axis=-1, keepdims=True) + 1e-05)


def normalize(v):
    c = v - jnp.mean(v, axis=-1, keepdims=True)
    return c * lax.rsqrt(jnp.mean(c * c, axis=-1, keepdims=True) + 1e-05)


def far_order(kind):
    j = iota((256, 256), 0)
    row = lax.bitwise_and(j, 1)
    if kind == 0:
        return lax.bitwise_and(lax.shift_right_logical(j, 1), 7) * 32 + lax.shift_right_logical(j, 4) * 2 + row
    return lax.bitwise_and(lax.shift_right_logical(j, 1), 15) * 16 + lax.shift_right_logical(j, 5) * 2 + row


def iota(shape, dim):
    return lax.broadcasted_iota(I32, shape, dim)


def hot(mask):
    return jnp.where(mask, 1.0, 0.0).astype(BF16)


def kernel(
    grid_hbm, send_ref, dest_ref, recv_ref, gfeat_ref, near_ref, far_ref, msend_ref, mrecv_ref, mfeat_ref,
    wgi_hbm, wef_ref, wmf_ref,
    wgo_h, wel_h, weo_h, wni_h, wno_h, wpe_h, wps_h, wpr_h, wpo_h, wus_h, wua_h, wuo_h,
    mesh_out, edge_out,
    idx, mrow_ref, graw, pick, gsel, wraw, wpad32, wgi, wts, aux, wefp, featp, wmf,
    eout, ein, scol, rcol, apre, apost, rmask, gsend,
    tpre, tnear, tfar, near_out, a1_out, a1_in, b1_out, b1_in, b2_out, b2_in, a2_out, a2_in, hbuf,
    pre, lat_buf, mbuf,
    in_sem, w_sem, es_sem, er_sem, ns_sem, nr_sem, a1s, a1r, b1s, b1r, b2s, b2r, a2s, a2r,
):
    lat = lax.axis_index("lat")
    lon = lax.axis_index("lon")
    zx = lax.div(lat, 2)
    core = lax.rem(lat, 2)
    spot = core * 4 + lon

    def near_id(code):
        return (
            lax.rem(lat + (code // 3 - 1) + N_LAT, N_LAT),
            lax.rem(lon + (code % 3 - 1) + N_LON, N_LON),
        )

    def a_peer(i):
        other = lax.rem(zx + i, 16)
        return other, (other * 2 + core, lon)

    def b_peer(i):
        other = lax.rem(spot + i, 8)
        return other, (zx * 2 + lax.div(other, 4), lax.rem(other, 4))

    barrier = pltpu.get_barrier_semaphore()
    for code in CODES:
        pl.semaphore_signal(barrier, inc=1, device_id=near_id(code), device_id_type=MESH)

    def greet_a(i, carry):
        pl.semaphore_signal(barrier, inc=1, device_id=a_peer(i)[1], device_id_type=MESH)
        return carry

    def greet_b(i, carry):
        pl.semaphore_signal(barrier, inc=1, device_id=b_peer(i)[1], device_id_type=MESH)
        return carry

    lax.fori_loop(1, 16, greet_a, 0)
    lax.fori_loop(1, 8, greet_b, 0)

    g_copy = pltpu.make_async_copy(grid_hbm, graw, in_sem.at[0])
    g_copy.start()
    wi_copy = pltpu.make_async_copy(wgi_hbm, wraw, in_sem.at[1])
    wi_copy.start()
    w_copies = {}
    for k, (name, ref) in enumerate(
        zip(W_NAMES, (wgo_h, wel_h, weo_h, wni_h, wno_h, wpe_h, wps_h, wpr_h, wpo_h, wus_h, wua_h, wuo_h))
    ):
        w_copies[name] = pltpu.make_async_copy(ref, wts.at[k], w_sem.at[k])
        w_copies[name].start()

    def weight(name):
        return wts[W_NAMES.index(name)]

    codes = dest_ref[...]
    marks = jnp.where(iota((16, EDGES), 0) == codes, 1.0, 0.0)
    below = hot(iota((EDGES, EDGES), 0) < iota((EDGES, EDGES), 1))
    earlier = dot(marks.astype(BF16), below)
    rank = jnp.sum(earlier * marks, axis=0, keepdims=True).astype(I32)
    place = codes * CAP + rank

    name_row = recv_ref[...].reshape(1, EDGES) + 1
    aux[...] = jnp.zeros_like(aux)
    aux[0:1, :] = lax.shift_right_logical(name_row, 4).astype(F32)
    aux[1:2, :] = lax.bitwise_and(name_row, 15).astype(F32)
    aux[4:8, :] = gfeat_ref[...].astype(F32)
    aux_rows = aux[...].astype(BF16)

    idx[COL_SEND : COL_SEND + 6, :] = send_ref[...].reshape(6, 128)
    for e in range(8):
        idx[COL_NEAR + e // 2 : COL_NEAR + e // 2 + 1, e % 2 * 64 : e % 2 * 64 + 64] = near_ref[e : e + 1, :]
    idx[COL_FAR : COL_FAR + 2, :] = far_ref[...]
    idx[COL_MS : COL_MS + 20, :] = msend_ref[...].reshape(20, 128)
    idx[COL_MR : COL_MR + 20, :] = mrecv_ref[...].reshape(20, 128)
    idx[COL_MR + 20 :, :] = jnp.zeros((128 - COL_MR - 20, 128), I32)
    mrow_ref[...] = mrecv_ref[...].reshape(1, MEDGES)
    idx_t = jnp.transpose(idx[...])

    g_copy.wait()
    gsel[:, 128:256] = jnp.zeros((EDGES, 128), BF16)
    for b in range(EDGES // 128):
        pick[b * 128 : (b + 1) * 128, :] = hot(idx_t[:, COL_SEND + b : COL_SEND + b + 1] == iota((128, GRID_N), 1))
    gsel[:, 0:CIN] = dot_nt(pick[...], graw[...]).astype(BF16)

    def choice(code):
        return hot(iota((CAP, EDGES), 0) + code * CAP == place)

    def pack(jobs):
        choose = jnp.concatenate([choice(code) for code, _, _ in jobs], axis=0)
        rows = dot(choose, gsel[...]).astype(BF16)
        tails = dot_nt(aux_rows, choose).astype(BF16)
        for i, (_, target, k) in enumerate(jobs):
            target[k, 0:CAP, :] = rows[i * CAP : (i + 1) * CAP]
            target[k, CAP:SLOT, :] = jnp.zeros((16, 256), BF16)
            target[k, CAP:SLOT, 0:CAP] = tails[:, i * CAP : (i + 1) * CAP]

    def edge_copy(k):
        return pltpu.make_async_remote_copy(
            src_ref=eout.at[k],
            dst_ref=ein.at[k],
            send_sem=es_sem.at[k],
            recv_sem=er_sem.at[k],
            device_id=near_id(CODES[k]),
            device_id_type=MESH,
        )

    for n in range(0, 8, 4):
        pack([(CODES[k], eout, k) for k in SEND_ORDER[n : n + 4]])
        if n == 0:
            pl.semaphore_wait(barrier, 8 + 15 + 7)
        for k in SEND_ORDER[n : n + 4]:
            edge_copy(k).start()
    pack([(4, ein, 8)])

    wi_copy.wait()
    wpad32[224:256, :] = jnp.zeros((32, L), F32)
    wpad32[0:CIN, :] = wraw[...].astype(F32)
    wgi[...] = wpad32[...].astype(BF16)
    wefp[...] = jnp.zeros_like(wefp)
    wefp[4:8, :] = wef_ref[...].astype(F32)

    def centre(name):
        w_copies[name].wait()
        w = weight(name).astype(F32)
        wts[W_NAMES.index(name)] = (w - jnp.mean(w, axis=-1, keepdims=True)).astype(BF16)

    centre("wgo")
    w_copies["wel"].wait()
    centre("weo")

    def encode(slots, count):
        wf = wefp[...].astype(BF16)
        tails = [slots[i, CAP:SLOT, :][:, 0:CAP] for i in range(count)]
        v = dot(slots[:, 0:CAP, :].reshape(count * CAP, 256), wgi[...])
        v = dot(silu(v).astype(BF16), weight("wgo"))
        v = dot(scaled(v).astype(BF16), weight("wel"))
        feat = [dot_tn(t, wf) for t in tails]
        v = v + (jnp.concatenate(feat, axis=0) if count > 1 else feat[0])
        message = scaled(dot(silu(v).astype(BF16), weight("weo"))).astype(BF16)
        total = None
        for i, t in enumerate(tails):
            t = t.astype(F32)
            node = (t[0:1, :] * 16.0 + t[1:2, :] - 1.0).astype(I32)
            part = dot(hot(iota((NODES, CAP), 0) == node), message[i * CAP : (i + 1) * CAP])
            total = part if total is None else total + part
        return total

    mbuf[...] = encode(ein[8:9], 1)

    for b in range(MEDGES // 128):
        scol[b] = jnp.broadcast_to(idx_t[:, COL_MS + b : COL_MS + b + 1], (128, 128))
        rcol[b] = jnp.broadcast_to(idx_t[:, COL_MR + b : COL_MR + b + 1], (128, 128))
    def node_hot(c):
        return hot(idx_t[:, c : c + 1] == iota((128, NODES), 1))

    for b in range(4):
        gsend[b * 128 : (b + 1) * 128, :] = node_hot(COL_NEAR + b)
    j = iota((256, 256), 0)
    k = iota((256, 256), 1)
    j_row = lax.bitwise_and(j, 1)
    j_zx = lax.bitwise_and(lax.shift_right_logical(j, 1), 15)
    j_spot = lax.shift_right_logical(j, 5)
    far_hot = jnp.concatenate([node_hot(COL_FAR), node_hot(COL_FAR + 1)], axis=0)
    gsend[512:768, :] = dot(hot(k == j_row * 128 + lax.shift_right_logical(j, 1)), far_hot).astype(BF16)
    gsend[768:1024, :] = dot(hot(k == j_row * 128 + j_zx * 8 + j_spot), far_hot).astype(BF16)

    featp[...] = jnp.zeros_like(featp)
    featp[0:4, :] = mfeat_ref[...].astype(F32)
    apre[:, 640:768] = jnp.zeros((MEDGES, 128), BF16)

    def masks(b, carry):
        s = scol[b]
        r = rcol[b]
        lane = iota((128, 128), 1)
        rows = pl.ds(pl.multiple_of(b * 128, 128), 128)
        for t in range(5):
            if t < 2:
                m = s == lane + t * 128
            elif t == 2:
                m = ((s == lane + 256) & (lane < 64)) | (r == lane - 64)
            else:
                m = r == lane + (t * 128 - NODES)
            apre[rows, t * 128 : (t + 1) * 128] = hot(m)
        for t in range(4):
            apost[rows, t * 128 : (t + 1) * 128] = hot(s == lane + (NODES + t * 128))
        f = s - (NODES + 8 * HCAP)
        for t in range(2):
            apost[rows, 512 + t * 128 : 512 + (t + 1) * 128] = hot(f == lane + t * 128)
        lanes = pl.ds(pl.multiple_of(b * 128, 128), 128)
        apre[rows, 640:648] = jnp.transpose(featp[:, lanes]).astype(BF16)
        rmask[:, lanes] = hot(iota((NODES, 128), 0) == mrow_ref[:, lanes])
        return carry

    lax.fori_loop(0, MEDGES // 128, masks, 0)

    centre("wpo")
    w_copies["wpe"].wait()
    wmf[...] = jnp.zeros_like(wmf)
    wmfp = jnp.concatenate([wmf_ref[...].astype(F32), jnp.zeros((12, L), F32)], axis=0).astype(BF16)
    wmf[0:16, :] = wmfp
    tpre[640:768, :] = jnp.zeros((128, L), BF16)
    tpre[640:656, :] = dot(wmfp, weight("wpe")).astype(BF16)

    def landed(k):
        return pltpu.make_async_remote_copy(
            src_ref=eout.at[k],
            dst_ref=ein.at[k],
            send_sem=es_sem.at[k],
            recv_sem=er_sem.at[k],
            device_id=near_id(CODES[0]),
            device_id_type=MESH,
        )

    def arrive(g, carry):
        for i in range(4):
            landed(4 * g + i).wait_recv()
        mbuf[...] += encode(ein[pl.ds(4 * g, 4)], 4)
        return carry

    lax.fori_loop(0, 2, arrive, 0)

    w_copies["wni"].wait()
    w_copies["wno"].wait()
    h = silu(dot(mbuf[...].astype(BF16), weight("wni"))).astype(BF16)
    latent = normalize(dot(h, weight("wno"))).astype(BF16)
    lat_buf[...] = latent
    w_copies["wps"].wait()
    own = dot(latent, weight("wps")).astype(BF16)
    tpre[0:NODES, :] = own

    def a1_copy(i):
        other, device = a_peer(i)
        return pltpu.make_async_remote_copy(
            src_ref=a1_out.at[other], dst_ref=a1_in.at[zx],
            send_sem=a1s.at[i], recv_sem=a1r.at[i], device_id=device, device_id_type=MESH,
        )

    def b1_copy(i):
        other, device = b_peer(i)
        return pltpu.make_async_remote_copy(
            src_ref=b1_out.at[other], dst_ref=b1_in.at[spot],
            send_sem=b1s.at[i], recv_sem=b1r.at[i], device_id=device, device_id_type=MESH,
        )

    def a2_copy(i):
        other, device = a_peer(i)
        return pltpu.make_async_remote_copy(
            src_ref=a2_out.at[other], dst_ref=a2_in.at[zx],
            send_sem=a2s.at[i], recv_sem=a2r.at[i], device_id=device, device_id_type=MESH,
        )

    def b2_copy(i):
        other, device = b_peer(i)
        return pltpu.make_async_remote_copy(
            src_ref=b2_out.at[other], dst_ref=b2_in.at[spot],
            send_sem=b2s.at[i], recv_sem=b2r.at[i], device_id=device, device_id_type=MESH,
        )

    def each(count, make, act):
        def step(i, carry):
            act(make(i))
            return carry

        lax.fori_loop(1, count, step, 0)

    def start(copy):
        copy.start()

    def arrived(copy):
        copy.wait_recv()

    def gone(copy):
        copy.wait_send()

    b1_out[...] = dot(gsend[768:1024, :], own[:, 256:512]).astype(BF16).reshape(8, 32, 256)
    each(8, b1_copy, start)
    a1_out[...] = dot(gsend[512:768, :], own[:, 0:256]).astype(BF16).reshape(16, 16, 256)
    each(16, a1_copy, start)

    def near_copy(e):
        return pltpu.make_async_remote_copy(
            src_ref=near_out.at[e],
            dst_ref=tnear.at[7 - e],
            send_sem=ns_sem.at[e],
            recv_sem=nr_sem.at[e],
            device_id=near_id(e if e < 4 else e + 1),
            device_id_type=MESH,
        )

    near_out[...] = dot(gsend[0:512, :], own).astype(BF16).reshape(8, HCAP, L)
    for e in (0, 2, 5, 7, 3, 4, 1, 6):
        near_copy(e).start()
    a1_in[zx] = a1_out[zx]
    b1_in[spot] = b1_out[spot]

    w_copies["wpr"].wait()
    tpre[NODES : 2 * NODES, :] = dot(latent, weight("wpr")).astype(BF16)

    def tall(b):
        return pl.ds(pl.multiple_of(b * TALL, TALL), TALL)

    def ahead(b, carry):
        edge_out[tall(b), :] = dot(apre[tall(b), 640:768], wmf[...]).astype(BF16)
        pre[tall(b), :] = dot(apre[tall(b), :], tpre[...])
        return carry

    ahead(0, 0)

    each(8, b1_copy, arrived)
    to_zx = hot(iota((256, 256), 1) == far_order(0))
    a2_out[...] = dot(to_zx, b1_in[...].reshape(256, 256)).astype(BF16).reshape(16, 16, 256)
    each(16, a2_copy, start)
    each(16, a1_copy, arrived)
    to_spot = hot(iota((256, 256), 1) == far_order(1))
    b2_out[...] = dot(to_spot, a1_in[...].reshape(256, 256)).astype(BF16).reshape(8, 32, 256)
    each(8, b2_copy, start)
    a2_in[zx] = a2_out[zx]
    b2_in[spot] = b2_out[spot]

    ahead(1, 0)

    for e in range(8):
        near_copy(e).wait_recv()

    def near_part(b, carry):
        pre[tall(b), :] += dot(apost[tall(b), 0:512], tnear[...].reshape(512, L))
        return carry

    lax.fori_loop(0, MEDGES // TALL, near_part, 0)

    each(16, a2_copy, arrived)
    each(8, b2_copy, arrived)
    tfar[:, 0:256] = dot(to_zx, b2_in[...].reshape(256, 256)).astype(BF16)
    tfar[:, 256:512] = a2_in[...].reshape(256, 256)

    mbuf[...] = jnp.zeros_like(mbuf)

    def hidden(b):
        rows = pl.ds(pl.multiple_of(b * BLK, BLK), BLK)
        return silu(pre[rows, :] + dot(apost[rows, 512:768], tfar[...])).astype(BF16)

    def finish(b, h):
        rows = pl.ds(pl.multiple_of(b * BLK, BLK), BLK)
        return (edge_out[rows, :].astype(F32) + scaled(dot(h, weight("wpo")))).astype(BF16)

    hbuf[0] = hidden(0)

    def process(b, carry):
        rows = pl.ds(pl.multiple_of(b * BLK, BLK), BLK)
        out = finish(b, hbuf[lax.rem(b, 2)])
        ahead_h = hidden(b + 1)
        total = mbuf[...] + dot(rmask[:, rows], out)
        edge_out[rows, :] = out
        hbuf[lax.rem(b + 1, 2)] = ahead_h
        mbuf[...] = total
        return carry

    lax.fori_loop(0, NBLK - 1, process, 0)
    last = NBLK - 1
    out = finish(last, hbuf[last % 2])
    edge_out[last * BLK : MEDGES, :] = out
    edge_sum = (mbuf[...] + dot(rmask[:, last * BLK : MEDGES], out)).astype(BF16)

    w_copies["wus"].wait()
    w_copies["wua"].wait()
    w_copies["wuo"].wait()
    h = dot(lat_buf[...], weight("wus")) + dot(edge_sum, weight("wua"))
    h = silu(h).astype(BF16)
    mesh_out[...] = (lat_buf[...].astype(F32) + normalize(dot(h, weight("wuo")))).astype(BF16)

    for k in range(8):
        edge_copy(k).wait_send()
        near_copy(k).wait_send()

    each(16, a1_copy, gone)
    each(8, b1_copy, gone)
    each(16, a2_copy, gone)
    each(8, b2_copy, gone)


def hand_out(mesh_from, edge_from, mesh_to, edge_to, sems):
    copies = [pltpu.make_async_copy(mesh_from, mesh_to, sems.at[0])]
    for b in range(PIECES):
        rows = pl.ds(b * (MEDGES // PIECES), MEDGES // PIECES)
        copies.append(pltpu.make_async_copy(edge_from.at[rows], edge_to.at[rows], sems.at[1 + b]))
    for copy in copies:
        copy.start()
    for copy in copies:
        copy.wait()


def on_device(
    grid_in, g2m_senders, g2m_dest, g2m_receivers, g2m_feat, halo_near, halo_far, mesh_senders,
    mesh_receivers, mesh_feat, w_grid_in, w_grid_out, w_edge_latent, w_edge_feat, w_edge_out, w_node_in,
    w_node_out, w_mesh_feat, w_proc_edge, w_proc_send, w_proc_recv, w_proc_out, w_upd_self, w_upd_sum,
    w_upd_out,
):
    vm = pl.BlockSpec(memory_space=pltpu.VMEM)
    hb = pl.BlockSpec(memory_space=pl.ANY)
    dma = pltpu.SemaphoreType.DMA
    mesh_rows, edge_rows = pl.pallas_call(
        kernel,
        out_shape=(
            pltpu.VMEM((NODES, L), BF16),
            pltpu.VMEM((MEDGES, L), BF16),
        ),
        in_specs=[hb, vm, vm, vm, vm, vm, vm, vm, vm, vm, hb, vm, vm] + [hb] * 12,
        out_specs=(vm, vm),
        scratch_shapes=[
            pltpu.VMEM((128, 128), I32),
            pltpu.VMEM((1, MEDGES), I32),
            pltpu.VMEM((CIN, GRID_N), BF16),
            pltpu.VMEM((EDGES, GRID_N), BF16),
            pltpu.VMEM((EDGES, 256), BF16),
            pltpu.VMEM((CIN, L), BF16),
            pltpu.VMEM((256, L), F32),
            pltpu.VMEM((256, L), BF16),
            pltpu.VMEM((12, L, L), BF16),
            pltpu.VMEM((16, EDGES), F32),
            pltpu.VMEM((16, L), F32),
            pltpu.VMEM((8, MEDGES), F32),
            pltpu.VMEM((128, L), BF16),
            pltpu.VMEM((8, SLOT, 256), BF16),
            pltpu.VMEM((9, SLOT, 256), BF16),
            pltpu.VMEM((MEDGES // 128, 128, 128), I32),
            pltpu.VMEM((MEDGES // 128, 128, 128), I32),
            pltpu.VMEM((MEDGES, 768), BF16),
            pltpu.VMEM((MEDGES, 768), BF16),
            pltpu.VMEM((NODES, MEDGES), BF16),
            pltpu.VMEM((1024, NODES), BF16),
            pltpu.VMEM((768, L), BF16),
            pltpu.VMEM((8, HCAP, L), BF16),
            pltpu.VMEM((256, L), BF16),
            pltpu.VMEM((8, HCAP, L), BF16),
            pltpu.VMEM((16, 16, 256), BF16),
            pltpu.VMEM((16, 16, 256), BF16),
            pltpu.VMEM((8, 32, 256), BF16),
            pltpu.VMEM((8, 32, 256), BF16),
            pltpu.VMEM((8, 32, 256), BF16),
            pltpu.VMEM((8, 32, 256), BF16),
            pltpu.VMEM((16, 16, 256), BF16),
            pltpu.VMEM((16, 16, 256), BF16),
            pltpu.VMEM((2, BLK, L), BF16),
            pltpu.VMEM((MEDGES, L), F32),
            pltpu.VMEM((NODES, L), BF16),
            pltpu.VMEM((NODES, L), F32),
            dma((2,)),
            dma((12,)),
            dma((8,)),
            dma((8,)),
            dma((8,)),
            dma((8,)),
            dma((16,)),
            dma((16,)),
            dma((8,)),
            dma((8,)),
            dma((8,)),
            dma((8,)),
            dma((16,)),
            dma((16,)),
        ],
        compiler_params=pltpu.CompilerParams(
            collective_id=0, has_side_effects=True, vmem_limit_bytes=54 * 1024 * 1024
        ),
        cost_estimate=pl.CostEstimate(flops=15_000_000_000, bytes_accessed=12_000_000, transcendentals=4_000_000),
    )(
        grid_in.T, g2m_senders, g2m_dest.reshape(1, EDGES), g2m_receivers, g2m_feat,
        halo_near.reshape(8, HCAP), halo_far.reshape(128, 2).T, mesh_senders, mesh_receivers, mesh_feat, w_grid_in, w_edge_feat, w_mesh_feat,
        w_grid_out, w_edge_latent, w_edge_out, w_node_in, w_node_out, w_proc_edge, w_proc_send, w_proc_recv,
        w_proc_out, w_upd_self, w_upd_sum, w_upd_out,
    )

    return pl.pallas_call(
        hand_out,
        out_shape=(
            jax.ShapeDtypeStruct((NODES, L), BF16),
            jax.ShapeDtypeStruct((MEDGES, L), BF16),
        ),
        in_specs=[vm, vm],
        out_specs=(hb, hb),
        scratch_shapes=[dma((1 + PIECES,))],
    )(mesh_rows, edge_rows)


def solution(mesh):
    both = ("lat", "lon")
    rows, flat, cube = P(both, None), P(both), P(both, None, None)
    return jax.shard_map(
        on_device,
        mesh=mesh,
        in_specs=(rows, flat, rows, flat, P(None, both), cube, cube, flat, flat, P(None, both)) + (P(),) * 15,
        out_specs=(rows, rows),
        check_vma=False,
    )
```

```python
import functools

import jax
import jax.numpy as jnp
from jax import lax
from jax.experimental import pallas as pl
from jax.experimental.pallas import tpu as pltpu
from jax.sharding import PartitionSpec as P

F32 = jnp.float32
BF16 = jnp.bfloat16
I32 = jnp.int32
MESH = pl.DeviceIdType.MESH

N_LAT, N_LON = 32, 4
L = 512
CIN = 227
GRID_N = 1024
EDGES = 768
NODES = 320
MEDGES = 2560
CAP = 192
HCAP = 64
SLOT = CAP + 16
TALL = 1280
BLK = 640
NBLK = MEDGES // BLK

CODES = (1, 7, 3, 5, 0, 2, 6, 8)
SEND_ORDER = (2, 3, 0, 1, 4, 5, 6, 7)

COL_SEND = 0
COL_NEAR = 6
COL_FAR = 10
COL_MS = 12
COL_MR = 32

W_NAMES = (
    "wgo", "wel", "weo", "wni", "wno", "wpe", "wps", "wpr", "wpo",
)


def dot(a, b):
    return jnp.dot(a, b, preferred_element_type=F32)


def dot_tn(a, b):
    return lax.dot_general(a, b, (((0,), (0,)), ((), ())), preferred_element_type=F32)


def dot_nt(a, b):
    return lax.dot_general(a, b, (((1,), (1,)), ((), ())), preferred_element_type=F32)


def silu(v):
    h = 0.5 * v
    return h + h * jnp.tanh(h)


def scaled(v):
    return v * lax.rsqrt(jnp.mean(v * v, axis=-1, keepdims=True) + 1e-05)


def normalize(v):
    c = v - jnp.mean(v, axis=-1, keepdims=True)
    return c * lax.rsqrt(jnp.mean(c * c, axis=-1, keepdims=True) + 1e-05)


def far_order(kind):
    j = iota((256, 256), 0)
    row = lax.bitwise_and(j, 1)
    if kind == 0:
        return lax.bitwise_and(lax.shift_right_logical(j, 1), 7) * 32 + lax.shift_right_logical(j, 4) * 2 + row
    return lax.bitwise_and(lax.shift_right_logical(j, 1), 15) * 16 + lax.shift_right_logical(j, 5) * 2 + row


def iota(shape, dim):
    return lax.broadcasted_iota(I32, shape, dim)


def hot(mask):
    return jnp.where(mask, 1.0, 0.0).astype(BF16)


def kernel(
    grid_hbm, send_ref, dest_ref, recv_ref, gfeat_ref, near_ref, far_ref, msend_ref, mrecv_ref, mfeat_ref,
    wgi_hbm, wef_ref, wmf_ref,
    wgo_h, wel_h, weo_h, wni_h, wno_h, wpe_h, wps_h, wpr_h, wpo_h,
    pre, embed_out, far_mask, rmask, tfar, lat_buf, wpo_out,
    idx, mrow_ref, graw, pick, gsel, wraw, wpad32, wgi, wts, aux, wefp, featp, wmf,
    eout, ein, scol, rcol, apre, apost, gsend,
    tpre, tnear, near_out, a1_out, a1_in, b1_out, b1_in, b2_out, b2_in, a2_out, a2_in, mbuf,
    in_sem, w_sem, es_sem, er_sem, ns_sem, nr_sem, a1s, a1r, b1s, b1r, b2s, b2r, a2s, a2r,
):
    lat = lax.axis_index("lat")
    lon = lax.axis_index("lon")
    zx = lax.div(lat, 2)
    core = lax.rem(lat, 2)
    spot = core * 4 + lon

    def near_id(code):
        return (
            lax.rem(lat + (code // 3 - 1) + N_LAT, N_LAT),
            lax.rem(lon + (code % 3 - 1) + N_LON, N_LON),
        )

    def a_peer(i):
        other = lax.rem(zx + i, 16)
        return other, (other * 2 + core, lon)

    def b_peer(i):
        other = lax.rem(spot + i, 8)
        return other, (zx * 2 + lax.div(other, 4), lax.rem(other, 4))

    barrier = pltpu.get_barrier_semaphore()
    for code in CODES:
        pl.semaphore_signal(barrier, inc=1, device_id=near_id(code), device_id_type=MESH)

    def greet_a(i, carry):
        pl.semaphore_signal(barrier, inc=1, device_id=a_peer(i)[1], device_id_type=MESH)
        return carry

    def greet_b(i, carry):
        pl.semaphore_signal(barrier, inc=1, device_id=b_peer(i)[1], device_id_type=MESH)
        return carry

    lax.fori_loop(1, 16, greet_a, 0)
    lax.fori_loop(1, 8, greet_b, 0)

    g_copy = pltpu.make_async_copy(grid_hbm, graw, in_sem.at[0])
    g_copy.start()
    wi_copy = pltpu.make_async_copy(wgi_hbm, wraw, in_sem.at[1])
    wi_copy.start()
    w_copies = {}
    for k, (name, ref) in enumerate(
        zip(W_NAMES, (wgo_h, wel_h, weo_h, wni_h, wno_h, wpe_h, wps_h, wpr_h, wpo_h))
    ):
        w_copies[name] = pltpu.make_async_copy(ref, wts.at[k], w_sem.at[k])
        w_copies[name].start()

    def weight(name):
        return wts[W_NAMES.index(name)]

    codes = dest_ref[...]
    marks = jnp.where(iota((16, EDGES), 0) == codes, 1.0, 0.0)
    below = hot(iota((EDGES, EDGES), 0) < iota((EDGES, EDGES), 1))
    earlier = dot(marks.astype(BF16), below)
    rank = jnp.sum(earlier * marks, axis=0, keepdims=True).astype(I32)
    place = codes * CAP + rank

    name_row = recv_ref[...].reshape(1, EDGES) + 1
    aux[...] = jnp.zeros_like(aux)
    aux[0:1, :] = lax.shift_right_logical(name_row, 4).astype(F32)
    aux[1:2, :] = lax.bitwise_and(name_row, 15).astype(F32)
    aux[4:8, :] = gfeat_ref[...].astype(F32)
    aux_rows = aux[...].astype(BF16)

    idx[COL_SEND : COL_SEND + 6, :] = send_ref[...].reshape(6, 128)
    for e in range(8):
        idx[COL_NEAR + e // 2 : COL_NEAR + e // 2 + 1, e % 2 * 64 : e % 2 * 64 + 64] = near_ref[e : e + 1, :]
    idx[COL_FAR : COL_FAR + 2, :] = far_ref[...]
    idx[COL_MS : COL_MS + 20, :] = msend_ref[...].reshape(20, 128)
    idx[COL_MR : COL_MR + 20, :] = mrecv_ref[...].reshape(20, 128)
    idx[COL_MR + 20 :, :] = jnp.zeros((128 - COL_MR - 20, 128), I32)
    mrow_ref[...] = mrecv_ref[...].reshape(1, MEDGES)
    idx_t = jnp.transpose(idx[...])

    g_copy.wait()
    gsel[:, 128:256] = jnp.zeros((EDGES, 128), BF16)
    for b in range(EDGES // 128):
        pick[b * 128 : (b + 1) * 128, :] = hot(idx_t[:, COL_SEND + b : COL_SEND + b + 1] == iota((128, GRID_N), 1))
    gsel[:, 0:CIN] = dot_nt(pick[...], graw[...]).astype(BF16)

    def choice(code):
        return hot(iota((CAP, EDGES), 0) + code * CAP == place)

    def pack(jobs):
        choose = jnp.concatenate([choice(code) for code, _, _ in jobs], axis=0)
        rows = dot(choose, gsel[...]).astype(BF16)
        tails = dot_nt(aux_rows, choose).astype(BF16)
        for i, (_, target, k) in enumerate(jobs):
            target[k, 0:CAP, :] = rows[i * CAP : (i + 1) * CAP]
            target[k, CAP:SLOT, :] = jnp.zeros((16, 256), BF16)
            target[k, CAP:SLOT, 0:CAP] = tails[:, i * CAP : (i + 1) * CAP]

    def edge_copy(k):
        return pltpu.make_async_remote_copy(
            src_ref=eout.at[k],
            dst_ref=ein.at[k],
            send_sem=es_sem.at[k],
            recv_sem=er_sem.at[k],
            device_id=near_id(CODES[k]),
            device_id_type=MESH,
        )

    for n in range(0, 8, 4):
        pack([(CODES[k], eout, k) for k in SEND_ORDER[n : n + 4]])
        if n == 0:
            pl.semaphore_wait(barrier, 8 + 15 + 7)
        for k in SEND_ORDER[n : n + 4]:
            edge_copy(k).start()
    pack([(4, ein, 8)])

    wi_copy.wait()
    wpad32[224:256, :] = jnp.zeros((32, L), F32)
    wpad32[0:CIN, :] = wraw[...].astype(F32)
    wgi[...] = wpad32[...].astype(BF16)
    wefp[...] = jnp.zeros_like(wefp)
    wefp[4:8, :] = wef_ref[...].astype(F32)

    def centre(name):
        w_copies[name].wait()
        w = weight(name).astype(F32)
        wts[W_NAMES.index(name)] = (w - jnp.mean(w, axis=-1, keepdims=True)).astype(BF16)

    centre("wgo")
    w_copies["wel"].wait()
    centre("weo")

    def encode(slots, count):
        wf = wefp[...].astype(BF16)
        tails = [slots[i, CAP:SLOT, :][:, 0:CAP] for i in range(count)]
        v = dot(slots[:, 0:CAP, :].reshape(count * CAP, 256), wgi[...])
        v = dot(silu(v).astype(BF16), weight("wgo"))
        v = dot(scaled(v).astype(BF16), weight("wel"))
        feat = [dot_tn(t, wf) for t in tails]
        v = v + (jnp.concatenate(feat, axis=0) if count > 1 else feat[0])
        message = scaled(dot(silu(v).astype(BF16), weight("weo"))).astype(BF16)
        total = None
        for i, t in enumerate(tails):
            t = t.astype(F32)
            node = (t[0:1, :] * 16.0 + t[1:2, :] - 1.0).astype(I32)
            part = dot(hot(iota((NODES, CAP), 0) == node), message[i * CAP : (i + 1) * CAP])
            total = part if total is None else total + part
        return total

    mbuf[...] = encode(ein[8:9], 1)

    for b in range(MEDGES // 128):
        scol[b] = jnp.broadcast_to(idx_t[:, COL_MS + b : COL_MS + b + 1], (128, 128))
        rcol[b] = jnp.broadcast_to(idx_t[:, COL_MR + b : COL_MR + b + 1], (128, 128))
    def node_hot(c):
        return hot(idx_t[:, c : c + 1] == iota((128, NODES), 1))

    for b in range(4):
        gsend[b * 128 : (b + 1) * 128, :] = node_hot(COL_NEAR + b)
    j = iota((256, 256), 0)
    k = iota((256, 256), 1)
    j_row = lax.bitwise_and(j, 1)
    j_zx = lax.bitwise_and(lax.shift_right_logical(j, 1), 15)
    j_spot = lax.shift_right_logical(j, 5)
    far_hot = jnp.concatenate([node_hot(COL_FAR), node_hot(COL_FAR + 1)], axis=0)
    gsend[512:768, :] = dot(hot(k == j_row * 128 + lax.shift_right_logical(j, 1)), far_hot).astype(BF16)
    gsend[768:1024, :] = dot(hot(k == j_row * 128 + j_zx * 8 + j_spot), far_hot).astype(BF16)

    featp[...] = jnp.zeros_like(featp)
    featp[0:4, :] = mfeat_ref[...].astype(F32)
    apre[:, 640:768] = jnp.zeros((MEDGES, 128), BF16)

    def masks(b, carry):
        s = scol[b]
        r = rcol[b]
        lane = iota((128, 128), 1)
        rows = pl.ds(pl.multiple_of(b * 128, 128), 128)
        for t in range(5):
            if t < 2:
                m = s == lane + t * 128
            elif t == 2:
                m = ((s == lane + 256) & (lane < 64)) | (r == lane - 64)
            else:
                m = r == lane + (t * 128 - NODES)
            apre[rows, t * 128 : (t + 1) * 128] = hot(m)
        for t in range(4):
            apost[rows, t * 128 : (t + 1) * 128] = hot(s == lane + (NODES + t * 128))
        f = s - (NODES + 8 * HCAP)
        for t in range(2):
            far_mask[rows, t * 128 : (t + 1) * 128] = hot(f == lane + t * 128)
        lanes = pl.ds(pl.multiple_of(b * 128, 128), 128)
        apre[rows, 640:648] = jnp.transpose(featp[:, lanes]).astype(BF16)
        rmask[:, lanes] = hot(iota((NODES, 128), 0) == mrow_ref[:, lanes])
        return carry

    lax.fori_loop(0, MEDGES // 128, masks, 0)

    centre("wpo")
    wpo_out[...] = weight("wpo")
    w_copies["wpe"].wait()
    wmf[...] = jnp.zeros_like(wmf)
    wmfp = jnp.concatenate([wmf_ref[...].astype(F32), jnp.zeros((12, L), F32)], axis=0).astype(BF16)
    wmf[0:16, :] = wmfp
    tpre[640:768, :] = jnp.zeros((128, L), BF16)
    tpre[640:656, :] = dot(wmfp, weight("wpe")).astype(BF16)

    def landed(k):
        return pltpu.make_async_remote_copy(
            src_ref=eout.at[k],
            dst_ref=ein.at[k],
            send_sem=es_sem.at[k],
            recv_sem=er_sem.at[k],
            device_id=near_id(CODES[0]),
            device_id_type=MESH,
        )

    def arrive(g, carry):
        for i in range(4):
            landed(4 * g + i).wait_recv()
        mbuf[...] += encode(ein[pl.ds(4 * g, 4)], 4)
        return carry

    lax.fori_loop(0, 2, arrive, 0)

    w_copies["wni"].wait()
    w_copies["wno"].wait()
    h = silu(dot(mbuf[...].astype(BF16), weight("wni"))).astype(BF16)
    latent = normalize(dot(h, weight("wno"))).astype(BF16)
    lat_buf[...] = latent
    w_copies["wps"].wait()
    own = dot(latent, weight("wps")).astype(BF16)
    tpre[0:NODES, :] = own

    def a1_copy(i):
        other, device = a_peer(i)
        return pltpu.make_async_remote_copy(
            src_ref=a1_out.at[other], dst_ref=a1_in.at[zx],
            send_sem=a1s.at[i], recv_sem=a1r.at[i], device_id=device, device_id_type=MESH,
        )

    def b1_copy(i):
        other, device = b_peer(i)
        return pltpu.make_async_remote_copy(
            src_ref=b1_out.at[other], dst_ref=b1_in.at[spot],
            send_sem=b1s.at[i], recv_sem=b1r.at[i], device_id=device, device_id_type=MESH,
        )

    def a2_copy(i):
        other, device = a_peer(i)
        return pltpu.make_async_remote_copy(
            src_ref=a2_out.at[other], dst_ref=a2_in.at[zx],
            send_sem=a2s.at[i], recv_sem=a2r.at[i], device_id=device, device_id_type=MESH,
        )

    def b2_copy(i):
        other, device = b_peer(i)
        return pltpu.make_async_remote_copy(
            src_ref=b2_out.at[other], dst_ref=b2_in.at[spot],
            send_sem=b2s.at[i], recv_sem=b2r.at[i], device_id=device, device_id_type=MESH,
        )

    def each(count, make, act):
        def step(i, carry):
            act(make(i))
            return carry

        lax.fori_loop(1, count, step, 0)

    def start(copy):
        copy.start()

    def arrived(copy):
        copy.wait_recv()

    def gone(copy):
        copy.wait_send()

    b1_out[...] = dot(gsend[768:1024, :], own[:, 256:512]).astype(BF16).reshape(8, 32, 256)
    each(8, b1_copy, start)
    a1_out[...] = dot(gsend[512:768, :], own[:, 0:256]).astype(BF16).reshape(16, 16, 256)
    each(16, a1_copy, start)

    def near_copy(e):
        return pltpu.make_async_remote_copy(
            src_ref=near_out.at[e],
            dst_ref=tnear.at[7 - e],
            send_sem=ns_sem.at[e],
            recv_sem=nr_sem.at[e],
            device_id=near_id(e if e < 4 else e + 1),
            device_id_type=MESH,
        )

    near_out[...] = dot(gsend[0:512, :], own).astype(BF16).reshape(8, HCAP, L)
    for e in (0, 2, 5, 7, 3, 4, 1, 6):
        near_copy(e).start()
    a1_in[zx] = a1_out[zx]
    b1_in[spot] = b1_out[spot]

    w_copies["wpr"].wait()
    tpre[NODES : 2 * NODES, :] = dot(latent, weight("wpr")).astype(BF16)

    def tall(b):
        return pl.ds(pl.multiple_of(b * TALL, TALL), TALL)

    def ahead(b, carry):
        embed_out[tall(b), :] = dot(apre[tall(b), 640:768], wmf[...]).astype(BF16)
        pre[tall(b), :] = dot(apre[tall(b), :], tpre[...])
        return carry

    ahead(0, 0)

    each(8, b1_copy, arrived)
    to_zx = hot(iota((256, 256), 1) == far_order(0))
    a2_out[...] = dot(to_zx, b1_in[...].reshape(256, 256)).astype(BF16).reshape(16, 16, 256)
    each(16, a2_copy, start)
    each(16, a1_copy, arrived)
    to_spot = hot(iota((256, 256), 1) == far_order(1))
    b2_out[...] = dot(to_spot, a1_in[...].reshape(256, 256)).astype(BF16).reshape(8, 32, 256)
    each(8, b2_copy, start)
    a2_in[zx] = a2_out[zx]
    b2_in[spot] = b2_out[spot]

    ahead(1, 0)

    for e in range(8):
        near_copy(e).wait_recv()

    def near_part(b, carry):
        pre[tall(b), :] += dot(apost[tall(b), 0:512], tnear[...].reshape(512, L))
        return carry

    lax.fori_loop(0, MEDGES // TALL, near_part, 0)

    each(16, a2_copy, arrived)
    each(8, b2_copy, arrived)
    tfar[:, 0:256] = dot(to_zx, b2_in[...].reshape(256, 256)).astype(BF16)
    tfar[:, 256:512] = a2_in[...].reshape(256, 256)

    for k in range(8):
        edge_copy(k).wait_send()
        near_copy(k).wait_send()

    each(16, a1_copy, gone)
    each(8, b1_copy, gone)
    each(16, a2_copy, gone)
    each(8, b2_copy, gone)


def finish_kernel(
    pre, embed, far_mask, rmask, tfar, lat_buf, wpo, wus_h, wua_h, wuo_h, mesh_out, edge_out,
    wts, obuf, hbuf, mbuf, w_sem, o_sem,
):
    w_copies = [pltpu.make_async_copy(ref, wts.at[k], w_sem.at[k]) for k, ref in enumerate((wus_h, wua_h, wuo_h))]
    for copy in w_copies:
        copy.start()

    def out_copy(b):
        rows = pl.ds(b * BLK, BLK)
        return pltpu.make_async_copy(obuf.at[rows], edge_out.at[rows], o_sem.at[b])

    def hidden(b):
        rows = pl.ds(b * BLK, BLK)
        return silu(pre[rows, :] + dot(far_mask[rows, :], tfar[...])).astype(BF16)

    def finish(b, h):
        rows = pl.ds(b * BLK, BLK)
        return (embed[rows, :].astype(F32) + scaled(dot(h, wpo[...]))).astype(BF16)

    mbuf[...] = jnp.zeros_like(mbuf)
    hbuf[0] = hidden(0)
    for b in range(NBLK):
        rows = pl.ds(b * BLK, BLK)
        out = finish(b, hbuf[b % 2])
        if b + 1 < NBLK:
            hbuf[(b + 1) % 2] = hidden(b + 1)
        obuf[rows, :] = out
        out_copy(b).start()
        mbuf[...] += dot(rmask[:, rows], out)

    for copy in w_copies:
        copy.wait()
    h = dot(lat_buf[...], wts[0]) + dot(mbuf[...].astype(BF16), wts[1])
    h = silu(h).astype(BF16)
    mesh_out[...] = (lat_buf[...].astype(F32) + normalize(dot(h, wts[2]))).astype(BF16)
    for b in range(NBLK):
        out_copy(b).wait()


def on_device(
    grid_in, g2m_senders, g2m_dest, g2m_receivers, g2m_feat, halo_near, halo_far, mesh_senders,
    mesh_receivers, mesh_feat, w_grid_in, w_grid_out, w_edge_latent, w_edge_feat, w_edge_out, w_node_in,
    w_node_out, w_mesh_feat, w_proc_edge, w_proc_send, w_proc_recv, w_proc_out, w_upd_self, w_upd_sum,
    w_upd_out,
):
    vm = pl.BlockSpec(memory_space=pltpu.VMEM)
    hb = pl.BlockSpec(memory_space=pl.ANY)
    dma = pltpu.SemaphoreType.DMA
    kept = pl.pallas_call(
        kernel,
        out_shape=(
            pltpu.VMEM((MEDGES, L), F32),
            pltpu.VMEM((MEDGES, L), BF16),
            pltpu.VMEM((MEDGES, 256), BF16),
            pltpu.VMEM((NODES, MEDGES), BF16),
            pltpu.VMEM((256, L), BF16),
            pltpu.VMEM((NODES, L), BF16),
            pltpu.VMEM((L, L), BF16),
        ),
        in_specs=[hb, vm, vm, vm, vm, vm, vm, vm, vm, vm, hb, vm, vm] + [hb] * 9,
        out_specs=(vm,) * 7,
        scratch_shapes=[
            pltpu.VMEM((128, 128), I32),
            pltpu.VMEM((1, MEDGES), I32),
            pltpu.VMEM((CIN, GRID_N), BF16),
            pltpu.VMEM((EDGES, GRID_N), BF16),
            pltpu.VMEM((EDGES, 256), BF16),
            pltpu.VMEM((CIN, L), BF16),
            pltpu.VMEM((256, L), F32),
            pltpu.VMEM((256, L), BF16),
            pltpu.VMEM((9, L, L), BF16),
            pltpu.VMEM((16, EDGES), F32),
            pltpu.VMEM((16, L), F32),
            pltpu.VMEM((8, MEDGES), F32),
            pltpu.VMEM((128, L), BF16),
            pltpu.VMEM((8, SLOT, 256), BF16),
            pltpu.VMEM((9, SLOT, 256), BF16),
            pltpu.VMEM((MEDGES // 128, 128, 128), I32),
            pltpu.VMEM((MEDGES // 128, 128, 128), I32),
            pltpu.VMEM((MEDGES, 768), BF16),
            pltpu.VMEM((MEDGES, 512), BF16),
            pltpu.VMEM((1024, NODES), BF16),
            pltpu.VMEM((768, L), BF16),
            pltpu.VMEM((8, HCAP, L), BF16),
            pltpu.VMEM((8, HCAP, L), BF16),
            pltpu.VMEM((16, 16, 256), BF16),
            pltpu.VMEM((16, 16, 256), BF16),
            pltpu.VMEM((8, 32, 256), BF16),
            pltpu.VMEM((8, 32, 256), BF16),
            pltpu.VMEM((8, 32, 256), BF16),
            pltpu.VMEM((8, 32, 256), BF16),
            pltpu.VMEM((16, 16, 256), BF16),
            pltpu.VMEM((16, 16, 256), BF16),
            pltpu.VMEM((NODES, L), F32),
            dma((2,)),
            dma((9,)),
            dma((8,)),
            dma((8,)),
            dma((8,)),
            dma((8,)),
            dma((16,)),
            dma((16,)),
            dma((8,)),
            dma((8,)),
            dma((8,)),
            dma((8,)),
            dma((16,)),
            dma((16,)),
        ],
        compiler_params=pltpu.CompilerParams(
            collective_id=0, has_side_effects=True, vmem_limit_bytes=44 * 1024 * 1024
        ),
        cost_estimate=pl.CostEstimate(flops=15_000_000_000, bytes_accessed=12_000_000, transcendentals=4_000_000),
    )(
        grid_in.T, g2m_senders, g2m_dest.reshape(1, EDGES), g2m_receivers, g2m_feat,
        halo_near.reshape(8, HCAP), halo_far.reshape(128, 2).T, mesh_senders, mesh_receivers, mesh_feat, w_grid_in, w_edge_feat, w_mesh_feat,
        w_grid_out, w_edge_latent, w_edge_out, w_node_in, w_node_out, w_proc_edge, w_proc_send, w_proc_recv,
        w_proc_out,
    )

    return pl.pallas_call(
        finish_kernel,
        out_shape=(
            jax.ShapeDtypeStruct((NODES, L), BF16),
            jax.ShapeDtypeStruct((MEDGES, L), BF16),
        ),
        in_specs=[vm] * 7 + [hb] * 3,
        out_specs=(vm, hb),
        scratch_shapes=[
            pltpu.VMEM((3, L, L), BF16),
            pltpu.VMEM((MEDGES, L), BF16),
            pltpu.VMEM((2, BLK, L), BF16),
            pltpu.VMEM((NODES, L), F32),
            dma((3,)),
            dma((NBLK,)),
        ],
        compiler_params=pltpu.CompilerParams(vmem_limit_bytes=20 * 1024 * 1024),
        cost_estimate=pl.CostEstimate(flops=4_000_000_000, bytes_accessed=5_000_000, transcendentals=1_500_000),
    )(*kept, w_upd_self, w_upd_sum, w_upd_out)


def solution(mesh):
    both = ("lat", "lon")
    rows, flat, cube = P(both, None), P(both), P(both, None, None)
    return jax.shard_map(
        on_device,
        mesh=mesh,
        in_specs=(rows, flat, rows, flat, P(None, both), cube, cube, flat, flat, P(None, both)) + (P(),) * 15,
        out_specs=(rows, rows),
        check_vma=False,
    )
```

```python
import functools

import jax
import jax.numpy as jnp
from jax import lax
from jax.experimental import pallas as pl
from jax.experimental.pallas import tpu as pltpu
from jax.sharding import PartitionSpec as P

F32 = jnp.float32
BF16 = jnp.bfloat16
I32 = jnp.int32
MESH = pl.DeviceIdType.MESH

N_LAT, N_LON = 32, 4
L = 512
CIN = 227
GRID_N = 1024
EDGES = 768
NODES = 320
MEDGES = 2560
CAP = 192
HCAP = 64
SLOT = CAP + 16
TALL = 1280
BLK = 1280
NBLK = MEDGES // BLK

CODES = (1, 7, 3, 5, 0, 2, 6, 8)
SEND_ORDER = (2, 3, 0, 1, 4, 5, 6, 7)

COL_SEND = 0
COL_NEAR = 6
COL_FAR = 10
COL_MS = 12
COL_MR = 32

W_NAMES = (
    "wgo", "wel", "weo", "wni", "wno", "wpe", "wps", "wpr", "wpo",
)


def dot(a, b):
    return jnp.dot(a, b, preferred_element_type=F32)


def dot_tn(a, b):
    return lax.dot_general(a, b, (((0,), (0,)), ((), ())), preferred_element_type=F32)


def dot_nt(a, b):
    return lax.dot_general(a, b, (((1,), (1,)), ((), ())), preferred_element_type=F32)


def silu(v):
    h = 0.5 * v
    return h + h * jnp.tanh(h)


def scaled(v):
    return v * lax.rsqrt(jnp.mean(v * v, axis=-1, keepdims=True) + 1e-05)


def normalize(v):
    c = v - jnp.mean(v, axis=-1, keepdims=True)
    return c * lax.rsqrt(jnp.mean(c * c, axis=-1, keepdims=True) + 1e-05)


def far_order(kind):
    j = iota((256, 256), 0)
    row = lax.bitwise_and(j, 1)
    if kind == 0:
        return lax.bitwise_and(lax.shift_right_logical(j, 1), 7) * 32 + lax.shift_right_logical(j, 4) * 2 + row
    return lax.bitwise_and(lax.shift_right_logical(j, 1), 15) * 16 + lax.shift_right_logical(j, 5) * 2 + row


def iota(shape, dim):
    return lax.broadcasted_iota(I32, shape, dim)


def hot(mask):
    return jnp.where(mask, 1.0, 0.0).astype(BF16)


def kernel(
    grid_hbm, send_ref, dest_ref, recv_ref, gfeat_ref, near_ref, far_ref, msend_ref, mrecv_ref, mfeat_ref,
    wgi_hbm, wef_ref, wmf_ref,
    wgo_h, wel_h, weo_h, wni_h, wno_h, wpe_h, wps_h, wpr_h, wpo_h,
    pre, embed_out, far_mask, rmask, tfar, lat_buf, wpo_out,
    idx, mrow_ref, graw, pick, gsel, wraw, wpad32, wgi, wts, aux, wefp, featp, wmf,
    eout, ein, scol, rcol, apre, apost, gsend,
    tpre, tnear, near_out, a1_out, a1_in, b1_out, b1_in, b2_out, b2_in, a2_out, a2_in, mbuf,
    in_sem, w_sem, es_sem, er_sem, ns_sem, nr_sem, a1s, a1r, b1s, b1r, b2s, b2r, a2s, a2r,
):
    lat = lax.axis_index("lat")
    lon = lax.axis_index("lon")
    zx = lax.div(lat, 2)
    core = lax.rem(lat, 2)
    spot = core * 4 + lon

    def near_id(code):
        return (
            lax.rem(lat + (code // 3 - 1) + N_LAT, N_LAT),
            lax.rem(lon + (code % 3 - 1) + N_LON, N_LON),
        )

    def a_peer(i):
        other = lax.rem(zx + i, 16)
        return other, (other * 2 + core, lon)

    def b_peer(i):
        other = lax.rem(spot + i, 8)
        return other, (zx * 2 + lax.div(other, 4), lax.rem(other, 4))

    barrier = pltpu.get_barrier_semaphore()
    for code in CODES:
        pl.semaphore_signal(barrier, inc=1, device_id=near_id(code), device_id_type=MESH)

    def greet_a(i, carry):
        pl.semaphore_signal(barrier, inc=1, device_id=a_peer(i)[1], device_id_type=MESH)
        return carry

    def greet_b(i, carry):
        pl.semaphore_signal(barrier, inc=1, device_id=b_peer(i)[1], device_id_type=MESH)
        return carry

    lax.fori_loop(1, 16, greet_a, 0)
    lax.fori_loop(1, 8, greet_b, 0)

    g_copy = pltpu.make_async_copy(grid_hbm, graw, in_sem.at[0])
    g_copy.start()
    wi_copy = pltpu.make_async_copy(wgi_hbm, wraw, in_sem.at[1])
    wi_copy.start()
    w_copies = {}
    for k, (name, ref) in enumerate(
        zip(W_NAMES, (wgo_h, wel_h, weo_h, wni_h, wno_h, wpe_h, wps_h, wpr_h, wpo_h))
    ):
        w_copies[name] = pltpu.make_async_copy(ref, wts.at[k], w_sem.at[k])
        w_copies[name].start()

    def weight(name):
        return wts[W_NAMES.index(name)]

    codes = dest_ref[...]
    marks = jnp.where(iota((16, EDGES), 0) == codes, 1.0, 0.0)
    below = hot(iota((EDGES, EDGES), 0) < iota((EDGES, EDGES), 1))
    earlier = dot(marks.astype(BF16), below)
    rank = jnp.sum(earlier * marks, axis=0, keepdims=True).astype(I32)
    place = codes * CAP + rank

    name_row = recv_ref[...].reshape(1, EDGES) + 1
    aux[...] = jnp.zeros_like(aux)
    aux[0:1, :] = lax.shift_right_logical(name_row, 4).astype(F32)
    aux[1:2, :] = lax.bitwise_and(name_row, 15).astype(F32)
    aux[4:8, :] = gfeat_ref[...].astype(F32)
    aux_rows = aux[...].astype(BF16)

    idx[COL_SEND : COL_SEND + 6, :] = send_ref[...].reshape(6, 128)
    for e in range(8):
        idx[COL_NEAR + e // 2 : COL_NEAR + e // 2 + 1, e % 2 * 64 : e % 2 * 64 + 64] = near_ref[e : e + 1, :]
    idx[COL_FAR : COL_FAR + 2, :] = far_ref[...]
    idx[COL_MS : COL_MS + 20, :] = msend_ref[...].reshape(20, 128)
    idx[COL_MR : COL_MR + 20, :] = mrecv_ref[...].reshape(20, 128)
    idx[COL_MR + 20 :, :] = jnp.zeros((128 - COL_MR - 20, 128), I32)
    mrow_ref[...] = mrecv_ref[...].reshape(1, MEDGES)
    idx_t = jnp.transpose(idx[...])

    g_copy.wait()
    gsel[:, 128:256] = jnp.zeros((EDGES, 128), BF16)
    for b in range(EDGES // 128):
        pick[b * 128 : (b + 1) * 128, :] = hot(idx_t[:, COL_SEND + b : COL_SEND + b + 1] == iota((128, GRID_N), 1))
    gsel[:, 0:CIN] = dot_nt(pick[...], graw[...]).astype(BF16)

    def choice(code):
        return hot(iota((CAP, EDGES), 0) + code * CAP == place)

    def pack(jobs):
        choose = jnp.concatenate([choice(code) for code, _, _ in jobs], axis=0)
        rows = dot(choose, gsel[...]).astype(BF16)
        tails = dot_nt(aux_rows, choose).astype(BF16)
        for i, (_, target, k) in enumerate(jobs):
            target[k, 0:CAP, :] = rows[i * CAP : (i + 1) * CAP]
            target[k, CAP:SLOT, :] = jnp.zeros((16, 256), BF16)
            target[k, CAP:SLOT, 0:CAP] = tails[:, i * CAP : (i + 1) * CAP]

    def edge_copy(k):
        return pltpu.make_async_remote_copy(
            src_ref=eout.at[k],
            dst_ref=ein.at[k],
            send_sem=es_sem.at[k],
            recv_sem=er_sem.at[k],
            device_id=near_id(CODES[k]),
            device_id_type=MESH,
        )

    for n in range(0, 8, 4):
        pack([(CODES[k], eout, k) for k in SEND_ORDER[n : n + 4]])
        if n == 0:
            pl.semaphore_wait(barrier, 8 + 15 + 7)
        for k in SEND_ORDER[n : n + 4]:
            edge_copy(k).start()
    pack([(4, ein, 8)])

    wi_copy.wait()
    wpad32[224:256, :] = jnp.zeros((32, L), F32)
    wpad32[0:CIN, :] = wraw[...].astype(F32)
    wgi[...] = wpad32[...].astype(BF16)
    wefp[...] = jnp.zeros_like(wefp)
    wefp[4:8, :] = wef_ref[...].astype(F32)

    def centre(name):
        w_copies[name].wait()
        w = weight(name).astype(F32)
        wts[W_NAMES.index(name)] = (w - jnp.mean(w, axis=-1, keepdims=True)).astype(BF16)

    centre("wgo")
    w_copies["wel"].wait()
    centre("weo")

    def encode(slots, count):
        wf = wefp[...].astype(BF16)
        tails = [slots[i, CAP:SLOT, :][:, 0:CAP] for i in range(count)]
        v = dot(slots[:, 0:CAP, :].reshape(count * CAP, 256), wgi[...])
        v = dot(silu(v).astype(BF16), weight("wgo"))
        v = dot(scaled(v).astype(BF16), weight("wel"))
        feat = [dot_tn(t, wf) for t in tails]
        v = v + (jnp.concatenate(feat, axis=0) if count > 1 else feat[0])
        message = scaled(dot(silu(v).astype(BF16), weight("weo"))).astype(BF16)
        total = None
        for i, t in enumerate(tails):
            t = t.astype(F32)
            node = (t[0:1, :] * 16.0 + t[1:2, :] - 1.0).astype(I32)
            part = dot(hot(iota((NODES, CAP), 0) == node), message[i * CAP : (i + 1) * CAP])
            total = part if total is None else total + part
        return total

    mbuf[...] = encode(ein[8:9], 1)

    for b in range(MEDGES // 128):
        scol[b] = jnp.broadcast_to(idx_t[:, COL_MS + b : COL_MS + b + 1], (128, 128))
        rcol[b] = jnp.broadcast_to(idx_t[:, COL_MR + b : COL_MR + b + 1], (128, 128))
    def node_hot(c):
        return hot(idx_t[:, c : c + 1] == iota((128, NODES), 1))

    for b in range(4):
        gsend[b * 128 : (b + 1) * 128, :] = node_hot(COL_NEAR + b)
    j = iota((256, 256), 0)
    k = iota((256, 256), 1)
    j_row = lax.bitwise_and(j, 1)
    j_zx = lax.bitwise_and(lax.shift_right_logical(j, 1), 15)
    j_spot = lax.shift_right_logical(j, 5)
    far_hot = jnp.concatenate([node_hot(COL_FAR), node_hot(COL_FAR + 1)], axis=0)
    gsend[512:768, :] = dot(hot(k == j_row * 128 + lax.shift_right_logical(j, 1)), far_hot).astype(BF16)
    gsend[768:1024, :] = dot(hot(k == j_row * 128 + j_zx * 8 + j_spot), far_hot).astype(BF16)

    featp[...] = jnp.zeros_like(featp)
    featp[0:4, :] = mfeat_ref[...].astype(F32)
    apre[:, 640:768] = jnp.zeros((MEDGES, 128), BF16)

    def masks(b, carry):
        s = scol[b]
        r = rcol[b]
        lane = iota((128, 128), 1)
        rows = pl.ds(pl.multiple_of(b * 128, 128), 128)
        for t in range(5):
            if t < 2:
                m = s == lane + t * 128
            elif t == 2:
                m = ((s == lane + 256) & (lane < 64)) | (r == lane - 64)
            else:
                m = r == lane + (t * 128 - NODES)
            apre[rows, t * 128 : (t + 1) * 128] = hot(m)
        for t in range(4):
            apost[rows, t * 128 : (t + 1) * 128] = hot(s == lane + (NODES + t * 128))
        f = s - (NODES + 8 * HCAP)
        for t in range(2):
            far_mask[rows, t * 128 : (t + 1) * 128] = hot(f == lane + t * 128)
        lanes = pl.ds(pl.multiple_of(b * 128, 128), 128)
        apre[rows, 640:648] = jnp.transpose(featp[:, lanes]).astype(BF16)
        rmask[:, lanes] = hot(iota((NODES, 128), 0) == mrow_ref[:, lanes])
        return carry

    lax.fori_loop(0, MEDGES // 128, masks, 0)

    centre("wpo")
    wpo_out[...] = weight("wpo")
    w_copies["wpe"].wait()
    wmf[...] = jnp.zeros_like(wmf)
    wmfp = jnp.concatenate([wmf_ref[...].astype(F32), jnp.zeros((12, L), F32)], axis=0).astype(BF16)
    wmf[0:16, :] = wmfp
    tpre[640:768, :] = jnp.zeros((128, L), BF16)
    tpre[640:656, :] = dot(wmfp, weight("wpe")).astype(BF16)

    def landed(k):
        return pltpu.make_async_remote_copy(
            src_ref=eout.at[k],
            dst_ref=ein.at[k],
            send_sem=es_sem.at[k],
            recv_sem=er_sem.at[k],
            device_id=near_id(CODES[0]),
            device_id_type=MESH,
        )

    def arrive(g, carry):
        for i in range(4):
            landed(4 * g + i).wait_recv()
        mbuf[...] += encode(ein[pl.ds(4 * g, 4)], 4)
        return carry

    lax.fori_loop(0, 2, arrive, 0)

    w_copies["wni"].wait()
    w_copies["wno"].wait()
    h = silu(dot(mbuf[...].astype(BF16), weight("wni"))).astype(BF16)
    latent = normalize(dot(h, weight("wno"))).astype(BF16)
    lat_buf[...] = latent
    w_copies["wps"].wait()
    own = dot(latent, weight("wps")).astype(BF16)
    tpre[0:NODES, :] = own

    def a1_copy(i):
        other, device = a_peer(i)
        return pltpu.make_async_remote_copy(
            src_ref=a1_out.at[other], dst_ref=a1_in.at[zx],
            send_sem=a1s.at[i], recv_sem=a1r.at[i], device_id=device, device_id_type=MESH,
        )

    def b1_copy(i):
        other, device = b_peer(i)
        return pltpu.make_async_remote_copy(
            src_ref=b1_out.at[other], dst_ref=b1_in.at[spot],
            send_sem=b1s.at[i], recv_sem=b1r.at[i], device_id=device, device_id_type=MESH,
        )

    def a2_copy(i):
        other, device = a_peer(i)
        return pltpu.make_async_remote_copy(
            src_ref=a2_out.at[other], dst_ref=a2_in.at[zx],
            send_sem=a2s.at[i], recv_sem=a2r.at[i], device_id=device, device_id_type=MESH,
        )

    def b2_copy(i):
        other, device = b_peer(i)
        return pltpu.make_async_remote_copy(
            src_ref=b2_out.at[other], dst_ref=b2_in.at[spot],
            send_sem=b2s.at[i], recv_sem=b2r.at[i], device_id=device, device_id_type=MESH,
        )

    def each(count, make, act):
        def step(i, carry):
            act(make(i))
            return carry

        lax.fori_loop(1, count, step, 0)

    def start(copy):
        copy.start()

    def arrived(copy):
        copy.wait_recv()

    def gone(copy):
        copy.wait_send()

    b1_out[...] = dot(gsend[768:1024, :], own[:, 256:512]).astype(BF16).reshape(8, 32, 256)
    each(8, b1_copy, start)
    a1_out[...] = dot(gsend[512:768, :], own[:, 0:256]).astype(BF16).reshape(16, 16, 256)
    each(16, a1_copy, start)

    def near_copy(e):
        return pltpu.make_async_remote_copy(
            src_ref=near_out.at[e],
            dst_ref=tnear.at[7 - e],
            send_sem=ns_sem.at[e],
            recv_sem=nr_sem.at[e],
            device_id=near_id(e if e < 4 else e + 1),
            device_id_type=MESH,
        )

    near_out[...] = dot(gsend[0:512, :], own).astype(BF16).reshape(8, HCAP, L)
    a1_in[zx] = a1_out[zx]
    b1_in[spot] = b1_out[spot]

    w_copies["wpr"].wait()
    tpre[NODES : 2 * NODES, :] = dot(latent, weight("wpr")).astype(BF16)

    def tall(b):
        return pl.ds(pl.multiple_of(b * TALL, TALL), TALL)

    def ahead(b, carry):
        embed_out[tall(b), :] = dot(apre[tall(b), 640:768], wmf[...]).astype(BF16)
        pre[tall(b), :] = dot(apre[tall(b), :], tpre[...])
        return carry

    ahead(0, 0)
    for e in (0, 2, 5, 7, 3, 4, 1, 6):
        near_copy(e).start()

    each(8, b1_copy, arrived)
    to_zx = hot(iota((256, 256), 1) == far_order(0))
    a2_out[...] = dot(to_zx, b1_in[...].reshape(256, 256)).astype(BF16).reshape(16, 16, 256)
    each(16, a2_copy, start)
    each(16, a1_copy, arrived)
    to_spot = hot(iota((256, 256), 1) == far_order(1))
    b2_out[...] = dot(to_spot, a1_in[...].reshape(256, 256)).astype(BF16).reshape(8, 32, 256)
    each(8, b2_copy, start)
    a2_in[zx] = a2_out[zx]
    b2_in[spot] = b2_out[spot]

    ahead(1, 0)

    for e in range(8):
        near_copy(e).wait_recv()

    def near_part(b, carry):
        pre[tall(b), :] += dot(apost[tall(b), 0:512], tnear[...].reshape(512, L))
        return carry

    lax.fori_loop(0, MEDGES // TALL, near_part, 0)

    each(16, a2_copy, arrived)
    each(8, b2_copy, arrived)
    tfar[:, 0:256] = dot(to_zx, b2_in[...].reshape(256, 256)).astype(BF16)
    tfar[:, 256:512] = a2_in[...].reshape(256, 256)

    for k in range(8):
        edge_copy(k).wait_send()
        near_copy(k).wait_send()

    each(16, a1_copy, gone)
    each(8, b1_copy, gone)
    each(16, a2_copy, gone)
    each(8, b2_copy, gone)


def finish_kernel(
    pre, embed, far_mask, rmask, tfar, lat_buf, wpo, wus_h, wua_h, wuo_h, mesh_out, edge_out,
    wts, obuf, hbuf, mbuf, w_sem, o_sem,
):
    w_copies = [pltpu.make_async_copy(ref, wts.at[k], w_sem.at[k]) for k, ref in enumerate((wus_h, wua_h, wuo_h))]
    for copy in w_copies:
        copy.start()

    def out_copy(b):
        rows = pl.ds(b * BLK, BLK)
        return pltpu.make_async_copy(obuf.at[rows], edge_out.at[rows], o_sem.at[b])

    def hidden(b):
        rows = pl.ds(b * BLK, BLK)
        return silu(pre[rows, :] + dot(far_mask[rows, :], tfar[...])).astype(BF16)

    def finish(b, h):
        rows = pl.ds(b * BLK, BLK)
        return (embed[rows, :].astype(F32) + scaled(dot(h, wpo[...]))).astype(BF16)

    mbuf[...] = jnp.zeros_like(mbuf)
    hbuf[0] = hidden(0)
    for b in range(NBLK):
        rows = pl.ds(b * BLK, BLK)
        out = finish(b, hbuf[b % 2])
        if b + 1 < NBLK:
            hbuf[(b + 1) % 2] = hidden(b + 1)
        obuf[rows, :] = out
        out_copy(b).start()
        mbuf[...] += dot(rmask[:, rows], out)

    for copy in w_copies:
        copy.wait()
    h = dot(lat_buf[...], wts[0]) + dot(mbuf[...].astype(BF16), wts[1])
    h = silu(h).astype(BF16)
    mesh_out[...] = (lat_buf[...].astype(F32) + normalize(dot(h, wts[2]))).astype(BF16)
    for b in range(NBLK):
        out_copy(b).wait()


def on_device(
    grid_in, g2m_senders, g2m_dest, g2m_receivers, g2m_feat, halo_near, halo_far, mesh_senders,
    mesh_receivers, mesh_feat, w_grid_in, w_grid_out, w_edge_latent, w_edge_feat, w_edge_out, w_node_in,
    w_node_out, w_mesh_feat, w_proc_edge, w_proc_send, w_proc_recv, w_proc_out, w_upd_self, w_upd_sum,
    w_upd_out,
):
    vm = pl.BlockSpec(memory_space=pltpu.VMEM)
    hb = pl.BlockSpec(memory_space=pl.ANY)
    dma = pltpu.SemaphoreType.DMA
    kept = pl.pallas_call(
        kernel,
        out_shape=(
            pltpu.VMEM((MEDGES, L), F32),
            pltpu.VMEM((MEDGES, L), BF16),
            pltpu.VMEM((MEDGES, 256), BF16),
            pltpu.VMEM((NODES, MEDGES), BF16),
            pltpu.VMEM((256, L), BF16),
            pltpu.VMEM((NODES, L), BF16),
            pltpu.VMEM((L, L), BF16),
        ),
        in_specs=[hb, vm, vm, vm, vm, vm, vm, vm, vm, vm, hb, vm, vm] + [hb] * 9,
        out_specs=(vm,) * 7,
        scratch_shapes=[
            pltpu.VMEM((128, 128), I32),
            pltpu.VMEM((1, MEDGES), I32),
            pltpu.VMEM((CIN, GRID_N), BF16),
            pltpu.VMEM((EDGES, GRID_N), BF16),
            pltpu.VMEM((EDGES, 256), BF16),
            pltpu.VMEM((CIN, L), BF16),
            pltpu.VMEM((256, L), F32),
            pltpu.VMEM((256, L), BF16),
            pltpu.VMEM((9, L, L), BF16),
            pltpu.VMEM((16, EDGES), F32),
            pltpu.VMEM((16, L), F32),
            pltpu.VMEM((8, MEDGES), F32),
            pltpu.VMEM((128, L), BF16),
            pltpu.VMEM((8, SLOT, 256), BF16),
            pltpu.VMEM((9, SLOT, 256), BF16),
            pltpu.VMEM((MEDGES // 128, 128, 128), I32),
            pltpu.VMEM((MEDGES // 128, 128, 128), I32),
            pltpu.VMEM((MEDGES, 768), BF16),
            pltpu.VMEM((MEDGES, 512), BF16),
            pltpu.VMEM((1024, NODES), BF16),
            pltpu.VMEM((768, L), BF16),
            pltpu.VMEM((8, HCAP, L), BF16),
            pltpu.VMEM((8, HCAP, L), BF16),
            pltpu.VMEM((16, 16, 256), BF16),
            pltpu.VMEM((16, 16, 256), BF16),
            pltpu.VMEM((8, 32, 256), BF16),
            pltpu.VMEM((8, 32, 256), BF16),
            pltpu.VMEM((8, 32, 256), BF16),
            pltpu.VMEM((8, 32, 256), BF16),
            pltpu.VMEM((16, 16, 256), BF16),
            pltpu.VMEM((16, 16, 256), BF16),
            pltpu.VMEM((NODES, L), F32),
            dma((2,)),
            dma((9,)),
            dma((8,)),
            dma((8,)),
            dma((8,)),
            dma((8,)),
            dma((16,)),
            dma((16,)),
            dma((8,)),
            dma((8,)),
            dma((8,)),
            dma((8,)),
            dma((16,)),
            dma((16,)),
        ],
        compiler_params=pltpu.CompilerParams(
            collective_id=0, has_side_effects=True, vmem_limit_bytes=44 * 1024 * 1024
        ),
        cost_estimate=pl.CostEstimate(flops=15_000_000_000, bytes_accessed=12_000_000, transcendentals=4_000_000),
    )(
        grid_in.T, g2m_senders, g2m_dest.reshape(1, EDGES), g2m_receivers, g2m_feat,
        halo_near.reshape(8, HCAP), halo_far.reshape(128, 2).T, mesh_senders, mesh_receivers, mesh_feat, w_grid_in, w_edge_feat, w_mesh_feat,
        w_grid_out, w_edge_latent, w_edge_out, w_node_in, w_node_out, w_proc_edge, w_proc_send, w_proc_recv,
        w_proc_out,
    )

    return pl.pallas_call(
        finish_kernel,
        out_shape=(
            jax.ShapeDtypeStruct((NODES, L), BF16),
            jax.ShapeDtypeStruct((MEDGES, L), BF16),
        ),
        in_specs=[vm] * 7 + [hb] * 3,
        out_specs=(vm, hb),
        scratch_shapes=[
            pltpu.VMEM((3, L, L), BF16),
            pltpu.VMEM((MEDGES, L), BF16),
            pltpu.VMEM((2, BLK, L), BF16),
            pltpu.VMEM((NODES, L), F32),
            dma((3,)),
            dma((NBLK,)),
        ],
        compiler_params=pltpu.CompilerParams(vmem_limit_bytes=20 * 1024 * 1024),
        cost_estimate=pl.CostEstimate(flops=4_000_000_000, bytes_accessed=5_000_000, transcendentals=1_500_000),
    )(*kept, w_upd_self, w_upd_sum, w_upd_out)


def solution(mesh):
    both = ("lat", "lon")
    rows, flat, cube = P(both, None), P(both), P(both, None, None)
    return jax.shard_map(
        on_device,
        mesh=mesh,
        in_specs=(rows, flat, rows, flat, P(None, both), cube, cube, flat, flat, P(None, both)) + (P(),) * 15,
        out_specs=(rows, rows),
        check_vma=False,
    )
```
